32 devices in a mesh: cluster: 4 (over z), seq: 8 (over y, x, core).
Axes of the slice: x: 2, y: 2, z: 4, core: 2. Of those that a mesh axis runs over, the one named last changes fastest.
Arguments:
- nodes: bfloat16 [16384, 1024], P(('cluster', 'seq')), may hold values from -48 to 48
- w_qkv: bfloat16 [1024, 3072], replicated, may hold values from -0.1875 to 0.1875
- w_out: bfloat16 [1024, 1024], replicated, may hold values from -1.5 to 1.5
- kv_ids: int32 [128, 16], P('cluster'), may hold values from 0 to 127, as said below
- counts: int32 [128], P('cluster'), may hold values from 13 to 16, as said below
Outputs:
- attended_out: bfloat16 [16384, 1024], P(('cluster', 'seq'))
The draws below stay inside these ranges and needn't reach their ends.
Inputs may be any that keep to these rules, and one draw needn't show every extreme that they name: `kv_ids`: entries name blocks; the cluster of block b is b // 32. For query block q, entry 0 is q itself, entries 0 to 11 are distinct blocks of q's cluster, and the last 4 entries are distinct blocks of other clusters. Over all entries of the query blocks of one cluster, at most 8 distinct blocks of any one other cluster are named, and exactly 8 for some pair of clusters. The first counts[q] entries of query block q's list are valid, the others are padding.
All inputs are finite; a program needn't handle non-finite values.
Results may differ from the reference program's by a relative error of at most 0.012.
Values may be sent and summed in bfloat16 or wider, within the bound.
No kernel may reach another device: no remote copies, remote signals or barrier semaphores. Data moves between devices by JAX's collectives and lax.ppermute only.
A program may use at most 128 MiB of HBM per device.

```python
import jax
import jax.numpy as jnp
from jax import lax

D = 1024
HEADS = 16
HD = 64
BLK = 128
KVB = 16
REMOTE = 4
QB_CL = 32
REQ = 8
CLUSTERS = 4
QBLOCKS = 128
NODES = 16384


def draw_lists(key):
    qrange = jnp.arange(QBLOCKS, dtype=jnp.int32)
    home = qrange // QB_CL
    inner = qrange % QB_CL
    row_keys = jax.random.split(jax.random.fold_in(key, 101), QBLOCKS)
    shuffled = jax.vmap(lambda k: jax.random.permutation(k, QB_CL - 1))(row_keys).astype(jnp.int32)
    others = (inner[:, None] + 1 + shuffled[:, :KVB - REMOTE - 1]) % QB_CL
    local_part = jnp.concatenate([inner[:, None], others], axis=1) + home[:, None] * QB_CL
    pool_keys = jax.random.split(jax.random.fold_in(key, 102), CLUSTERS * CLUSTERS)
    pools = jax.vmap(lambda k: jax.random.permutation(k, QB_CL))(pool_keys)[:, :REQ].astype(jnp.int32)
    pools = pools.reshape(CLUSTERS, CLUSTERS, REQ)
    offset = jax.random.randint(jax.random.fold_in(key, 103), (QBLOCKS, REMOTE), 1, CLUSTERS).astype(jnp.int32)
    first_off = jnp.where(inner < REQ, 1, offset[:, 0])
    offset = jnp.concatenate([first_off[:, None], offset[:, 1:]], axis=1)
    peer_ids = (home[:, None] + offset) % CLUSTERS
    start = jax.random.randint(jax.random.fold_in(key, 104), (QBLOCKS,), 0, REQ).astype(jnp.int32)
    start = jnp.where(inner < REQ, inner, start)
    pool_pos = (start[:, None] + jnp.arange(REMOTE, dtype=jnp.int32)[None, :]) % REQ
    remote_part = pools[home[:, None], peer_ids, pool_pos] + peer_ids * QB_CL
    lists = jnp.concatenate([local_part, remote_part], axis=1).astype(jnp.int32)
    drawn = jax.random.randint(jax.random.fold_in(key, 105), (QBLOCKS,), KVB - REMOTE + 1, KVB + 1).astype(jnp.int32)
    drawn = jnp.where(inner == 0, KVB, drawn).astype(jnp.int32)
    return (lists, drawn)


def draw_kv_ids(key, part):
    return draw_lists(key)[0]


def draw_counts(key, part):
    return draw_lists(key)[1]


def draw_nodes(key, part):
    values = jnp.clip(jax.random.normal(jax.random.fold_in(key, 7), (NODES, D), jnp.float32), -4.0, 4.0)
    return values.astype(jnp.bfloat16)


def noise(stream_key, dims, spread, most, kind=jnp.bfloat16):
    return jnp.clip(spread * jax.random.normal(stream_key, dims, jnp.float32), -most, most).astype(kind)


def setup_inputs(seed: int = 0) -> dict:
    key_of = jax.random.split(jax.random.key(seed), 6)
    return {
        "nodes": draw_nodes(jax.random.fold_in(key_of[5], 71), 0),
        "w_qkv": noise(key_of[1], (D, 3 * D), D ** -0.5, 0.1875),
        "w_out": noise(key_of[2], (D, D), KVB ** -0.5, 1.5),
        "kv_ids": draw_kv_ids(jax.random.fold_in(key_of[5], 71), 0),
        "counts": draw_counts(jax.random.fold_in(key_of[5], 71), 0),
    }


def reference(nodes, w_qkv, w_out, kv_ids, counts):
    projected = jnp.dot(nodes, w_qkv, preferred_element_type=jnp.float32).astype(jnp.bfloat16)
    blocks = projected.reshape(QBLOCKS, BLK, HEADS, 3, HD)
    queries = blocks[:, :, :, 0]
    keyvals = blocks[:, :, :, 1:]
    groups = QBLOCKS // 4
    slot_ids = jnp.arange(KVB, dtype=jnp.int32)

    def attend(packed):
        query_blk, block_ids, count_blk = packed
        gathered = keyvals[block_ids]
        key_part = gathered[:, :, :, :, 0].astype(jnp.float32)
        value_part = gathered[:, :, :, :, 1].astype(jnp.float32)
        scores = jnp.einsum('qahe,qjkhe->qhajk', query_blk.astype(jnp.float32), key_part) * (HD ** -0.5)
        is_valid = (slot_ids[None, :] < count_blk[:, None])[:, None, None, :, None]
        scores = jnp.where(is_valid, scores, -1e30)
        row_top = jnp.max(scores, axis=(3, 4), keepdims=True)
        exp_scores = jnp.exp(scores - row_top)
        row_total = jnp.sum(exp_scores, axis=(3, 4), keepdims=True)
        weight = (exp_scores / row_total).astype(jnp.bfloat16)
        return jnp.einsum('qhajk,qjkhe->qahe', weight.astype(jnp.float32), value_part).astype(jnp.bfloat16)

    attended = lax.map(attend, (queries.reshape(groups, 4, BLK, HEADS, HD), kv_ids.reshape(groups, 4, KVB), counts.reshape(groups, 4)))
    attended = attended.reshape(QBLOCKS * BLK, HEADS * HD)
    return jnp.dot(attended, w_out, preferred_element_type=jnp.float32).astype(jnp.bfloat16)
```

```python
import functools

import jax
import jax.numpy as jnp
from jax import lax
from jax.experimental import pallas as pl
from jax.experimental.pallas import tpu as pltpu
from jax.sharding import PartitionSpec as P

D = 1024
HEADS = 16
HD = 64
BLK = 128
KVB = 16
REMOTE = 4
NEAR = KVB - REMOTE
LOG2E = 1.4426950408889634
F32 = jnp.float32
BF16 = jnp.bfloat16

ANY = pl.BlockSpec(memory_space=pl.ANY)
SMEM = pl.BlockSpec(memory_space=pltpu.SMEM)
VMEM = pl.BlockSpec(memory_space=pltpu.VMEM)


def params():
    return pltpu.CompilerParams(vmem_limit_bytes=44 * 1024 * 1024)


def cost(flops, byts, trans=0):
    return pl.CostEstimate(flops=flops, bytes_accessed=byts, transcendentals=trans)


def nt_dot(a, b):
    return lax.dot_general(a, b, (((1,), (1,)), ((), ())), preferred_element_type=F32)


def project(parts, heads_dev, npair, meta, own, other, w_qkv):
    rows = own.shape[0]
    group = 3 * HD * heads_dev
    shared = group % 128 != 0
    slab = 2 * group if shared else group
    top = slab if shared else max(s + n for part in parts for s, n in part)
    width = -(-top // 128) * 128
    heights = [sum(n for _, n in part) for part in parts]
    total = sum(heights)

    def body(meta_ref, own_ref, other_ref, w_ref, *refs):
        outs = refs[: len(parts) * npair]
        x, w, wt, turned, sems = refs[len(parts) * npair :]
        pair = meta_ref[0]
        core = meta_ref[1]
        loads = []
        for j in range(npair):
            dest = pair ^ j
            start = dest * slab if shared else (2 * dest + core) * slab
            loads.append(
                pltpu.make_async_copy(
                    w_ref.at[:, pl.ds(pl.multiple_of(start, 128), width)], w.at[j], sems.at[j]
                )
            )
        here = pl.multiple_of(core * rows, 128)
        there = pl.multiple_of((1 - core) * rows, 128)
        loads.append(pltpu.make_async_copy(own_ref, x.at[pl.ds(here, rows)], sems.at[npair]))
        loads.append(pltpu.make_async_copy(other_ref, x.at[pl.ds(there, rows)], sems.at[npair + 1]))
        for load in loads:
            load.start()
        for j in range(npair):
            loads[j].wait()
            if shared:
                turned[...] = w[j].T
            else:
                full = w[j].T
            at = j * total
            for part in parts:
                for s, n in part:
                    if shared:
                        off = pl.multiple_of(core * group + s, HD)
                        wt[at : at + n, :] = turned[pl.ds(off, n), :]
                    else:
                        wt[at : at + n, :] = full[s : s + n, :]
                    at += n
        loads[npair].wait()
        loads[npair + 1].wait()
        step = 256
        for r in range(0, 2 * rows, step):
            res = nt_dot(wt[...], x[r : r + step, :]).astype(BF16)
            for j in range(npair):
                at = j * total
                for k in range(len(parts)):
                    outs[k * npair + j][:, r : r + step] = res[at : at + heights[k], :]
                    at += heights[k]

    shapes = [jax.ShapeDtypeStruct((heights[k], 2 * rows), BF16) for k in range(len(parts)) for _ in range(npair)]
    outs = pl.pallas_call(
        body,
        out_shape=shapes,
        in_specs=[SMEM, ANY, ANY, ANY],
        out_specs=[VMEM] * len(shapes),
        scratch_shapes=[
            pltpu.VMEM((2 * rows, D), BF16),
            pltpu.VMEM((npair, D, width), BF16),
            pltpu.VMEM((npair * total, D), BF16),
            pltpu.VMEM((width, D) if shared else (16, 128), BF16),
            pltpu.SemaphoreType.DMA((npair + 2,)),
        ],
        compiler_params=params(),
        cost_estimate=cost(2 * 2 * rows * D * total * npair, 4 * rows * D + 2 * D * width * npair),
        name="project",
    )(meta, own, other, w_qkv)
    return [list(outs[k * npair : (k + 1) * npair]) for k in range(len(parts))]


def select(npair, ncl, cap, meta, asked, tables):
    wide = tables[0].shape[1]
    per = wide // BLK

    def body(meta_ref, asked_ref, *refs):
        tabs = refs[:npair]
        outs = refs[npair : npair + ncl - 1]
        held, in_sems, out_sems = refs[npair + ncl - 1 :]
        pair = meta_ref[0]
        cluster = meta_ref[2]
        loads = [
            pltpu.make_async_copy(tabs[j], held.at[pair ^ j], in_sems.at[j]) for j in range(npair)
        ]
        for load in loads:
            load.start()
        for load in loads:
            load.wait()
        sends = []
        for s in range(1, ncl):
            dest = lax.rem(cluster + s, ncl)
            for i in range(cap):
                block = asked_ref[dest * cap + i]
                lane = pl.multiple_of(lax.rem(block, per) * BLK, BLK)
                sends.append(
                    pltpu.make_async_copy(
                        held.at[block // per, :, pl.ds(lane, BLK)],
                        outs[s - 1].at[i],
                        out_sems.at[(s - 1) * cap + i],
                    )
                )
        for send in sends:
            send.start()
        for send in sends:
            send.wait()

    shape = jax.ShapeDtypeStruct((cap, 2 * HD, BLK), BF16)
    return pl.pallas_call(
        body,
        out_shape=[shape] * (ncl - 1),
        in_specs=[SMEM, SMEM] + [ANY] * npair,
        out_specs=[ANY] * (ncl - 1),
        scratch_shapes=[
            pltpu.VMEM((npair, 2 * HD, wide), BF16),
            pltpu.SemaphoreType.DMA((npair,)),
            pltpu.SemaphoreType.DMA(((ncl - 1) * cap,)),
        ],
        compiler_params=params(),
        cost_estimate=cost(0, 4 * npair * 2 * HD * wide),
        name="select",
    )(meta, asked, *tables)


def near_attention(heads_dev, npair, meta, ids, tables, queries):
    wide = queries[0].shape[1]
    per = wide // BLK
    nblk = npair * per
    feats = heads_dev * HD
    cols = heads_dev * BLK
    keys = NEAR * BLK

    def body(meta_ref, ids_ref, *refs):
        tabs = refs[: npair * heads_dev]
        qs = refs[npair * heads_dev : npair * (heads_dev + 1)]
        out_ref, stat_ref, kv, q, ktab, vtab, s_a, s_b, sems = refs[npair * (heads_dev + 1) :]
        pair = meta_ref[0]
        loads = []
        for h in range(heads_dev):
            for j in range(npair):
                k = h * npair + j
                loads.append(pltpu.make_async_copy(tabs[k], kv.at[h, pair ^ j], sems.at[k]))
        for j in range(npair):
            loads.append(
                pltpu.make_async_copy(qs[j], q.at[pair ^ j], sems.at[heads_dev * npair + j])
            )
        for load in loads:
            load.start()
        for load in loads:
            load.wait()

        def build(p, carry):
            for i in range(per):
                at = slice(i * BLK, (i + 1) * BLK)
                pieces = [kv[h, p, :, at] for h in range(heads_dev)]
                if heads_dev == 1:
                    ktab[p * per + i] = pieces[0].T
                else:
                    ktab[p * per + i] = jnp.concatenate([x[:HD] for x in pieces], axis=0).T
                vtab[p * per + i] = jnp.concatenate([x[HD:] for x in pieces], axis=0)
            return carry

        lax.fori_loop(0, npair, build, 0)

        def first(b, held):
            lane = pl.multiple_of(lax.rem(b, per) * BLK, BLK)
            qt = q[b // per, :, pl.ds(lane, BLK)] * jnp.asarray(HD**-0.5, BF16)
            zero = jnp.zeros((HD, BLK), BF16)
            if heads_dev == 1:
                qm = jnp.concatenate([qt, zero], axis=0)
            else:
                qm = jnp.concatenate(
                    [
                        jnp.concatenate([qt[:HD], zero], axis=1),
                        jnp.concatenate([zero, qt[HD:]], axis=1),
                    ],
                    axis=0,
                )
            top = None
            for j in range(NEAR):
                s = jnp.dot(ktab[ids_ref[b * NEAR + j]], qm, preferred_element_type=F32)
                held[j * BLK : (j + 1) * BLK, :] = s
                part = jnp.max(s.reshape(BLK // 8, 8, cols), axis=0)
                top = part if top is None else jnp.maximum(top, part)
            return jnp.max(top, axis=0, keepdims=True)

        def second(b, held, top):
            acc = None
            total = None
            for c in range(0, NEAR, 4):
                p = jnp.exp2((held[c * BLK : (c + 4) * BLK, :] - top) * LOG2E)
                part = jnp.sum(p.reshape(4 * BLK // 8, 8, cols), axis=0)
                total = part if total is None else total + part
                v = jnp.concatenate([vtab[ids_ref[b * NEAR + c + i]] for i in range(4)], axis=1)
                o = jnp.dot(v, p.astype(BF16), preferred_element_type=F32)
                acc = o if acc is None else acc + o
            out_ref[b] = jnp.concatenate(
                [
                    acc[h * HD : (h + 1) * HD, h * BLK : (h + 1) * BLK]
                    for h in range(heads_dev)
                ],
                axis=0,
            )
            stat_ref[b, 0:1, :] = top
            stat_ref[b, 1:2, :] = jnp.sum(total, axis=0, keepdims=True)

        def step(i, top):
            b = 2 * i
            top_b = first(b + 1, s_b)
            second(b, s_a, top)
            top_a = first(jnp.minimum(b + 2, nblk - 1), s_a)
            second(b + 1, s_b, top_b)
            return top_a

        lax.fori_loop(0, nblk // 2, step, first(0, s_a))

    flops = nblk * keys * BLK * feats * 4 * heads_dev
    return pl.pallas_call(
        body,
        out_shape=[
            jax.ShapeDtypeStruct((nblk, feats, BLK), F32),
            jax.ShapeDtypeStruct((nblk, 8, cols), F32),
        ],
        in_specs=[SMEM, SMEM] + [ANY] * (npair * (heads_dev + 1)),
        out_specs=[VMEM, VMEM],
        scratch_shapes=[
            pltpu.VMEM((heads_dev, npair, 2 * HD, wide), BF16),
            pltpu.VMEM((npair, feats, wide), BF16),
            pltpu.VMEM((nblk, BLK, 2 * HD), BF16),
            pltpu.VMEM((nblk, feats, BLK), BF16),
            pltpu.VMEM((keys, cols), F32),
            pltpu.VMEM((keys, cols), F32),
            pltpu.SemaphoreType.DMA((npair * (heads_dev + 1),)),
        ],
        compiler_params=params(),
        cost_estimate=cost(2 * flops, 8 * nblk * BLK * feats, nblk * keys * cols),
        name="near_attention",
    )(meta, ids, *tables, *queries)


def far_attention(head, heads_dev, npair, seq_size, ncl, cap, meta, pos, counts, tables, queries, near, stats):
    wide = queries[0].shape[1]
    per = wide // BLK
    nblk = npair * per
    dev_blocks = nblk // seq_size
    feats = heads_dev * HD
    low = head * HD

    def body(meta_ref, pos_ref, counts_ref, *refs):
        tabs = refs[: ncl - 1]
        qs = refs[ncl - 1 : ncl - 1 + npair]
        near_ref, stat_ref = refs[ncl - 1 + npair : ncl + 1 + npair]
        outs = refs[ncl + 1 + npair : ncl + 1 + npair + seq_size]
        kv, q, ktab, o, sems = refs[ncl + 1 + npair + seq_size :]
        pair = meta_ref[0]
        cluster = meta_ref[2]
        seq = meta_ref[3]
        loads = []
        for s in range(1, ncl):
            origin = lax.rem(cluster + ncl - s, ncl)
            loads.append(
                pltpu.make_async_copy(
                    tabs[s - 1], kv.at[pl.ds(origin * cap, cap)], sems.at[s - 1]
                )
            )
        for j in range(npair):
            loads.append(
                pltpu.make_async_copy(
                    qs[j].at[pl.ds(low, HD)], q.at[pair ^ j], sems.at[ncl - 1 + j]
                )
            )
        loads.append(
            pltpu.make_async_copy(near_ref.at[:, pl.ds(low, HD), :], o, sems.at[ncl - 1 + npair])
        )
        for load in loads:
            load.start()
        for load in loads:
            load.wait()

        def build(s, carry):
            origin = lax.rem(cluster + ncl - s, ncl) * cap
            for i in range(cap):
                ktab[origin + i] = kv[origin + i].T
            return carry

        lax.fori_loop(1, ncl, build, 0)

        def block(b):
            lane = pl.multiple_of(lax.rem(b, per) * BLK, BLK)
            qt = q[b // per, :, pl.ds(lane, BLK)] * jnp.asarray(HD**-0.5, BF16)
            qm = jnp.concatenate([qt, jnp.zeros((HD, BLK), BF16)], axis=0)
            valid = counts_ref[b] - NEAR
            scores = []
            top = stat_ref[b, 0:1, low * 2 : low * 2 + BLK]
            was = top
            for j in range(REMOTE):
                s = jnp.dot(ktab[pos_ref[b * REMOTE + j]], qm, preferred_element_type=F32)
                s = jnp.where(j < valid, s, -1e30)
                scores.append(s)
                top = jnp.maximum(top, jnp.max(s, axis=0, keepdims=True))
            p = jnp.exp2((jnp.concatenate(scores, axis=0) - top) * LOG2E)
            fade = jnp.exp2((was - top) * LOG2E)
            total = stat_ref[b, 1:2, low * 2 : low * 2 + BLK] * fade + jnp.sum(p, axis=0, keepdims=True)
            v = jnp.concatenate([kv[pos_ref[b * REMOTE + j], HD:, :] for j in range(REMOTE)], axis=1)
            acc = jnp.dot(v, p.astype(BF16), preferred_element_type=F32)
            return ((acc + o[b] * fade) / total).astype(BF16)

        for k in range(seq_size):
            first = (seq ^ k) * dev_blocks
            for i in range(dev_blocks):
                outs[k][:, i * BLK : (i + 1) * BLK] = block(first + i)

    keys = REMOTE * BLK
    flops = nblk * keys * BLK * HD * 4
    return pl.pallas_call(
        body,
        out_shape=[jax.ShapeDtypeStruct((HD, dev_blocks * BLK), BF16)] * seq_size,
        in_specs=[SMEM, SMEM, SMEM] + [ANY] * (ncl - 1 + npair) + [ANY, VMEM],
        out_specs=[VMEM] * seq_size,
        scratch_shapes=[
            pltpu.VMEM((ncl * cap, 2 * HD, BLK), BF16),
            pltpu.VMEM((npair, HD, wide), BF16),
            pltpu.VMEM((ncl * cap, BLK, 2 * HD), BF16),
            pltpu.VMEM((nblk, HD, BLK), F32),
            pltpu.SemaphoreType.DMA((ncl + npair,)),
        ],
        compiler_params=params(),
        cost_estimate=cost(2 * flops, 6 * nblk * BLK * HD, nblk * keys * BLK),
        name="far_attention",
    )(meta, pos, counts, *tables, *queries, near, stats)


def project_out(heads_dev, seq_size, meta, pieces, w_out):
    rows = pieces[0][0].shape[1]

    def body(meta_ref, *refs):
        parts = refs[: heads_dev * seq_size]
        w_ref, out_ref, at, sems = refs[heads_dev * seq_size :]
        seq = meta_ref[3]
        loads = []
        for h in range(heads_dev):
            for k in range(seq_size):
                row = pl.multiple_of(((seq ^ k) * heads_dev + h) * HD, HD)
                n = h * seq_size + k
                loads.append(pltpu.make_async_copy(parts[n], at.at[pl.ds(row, HD)], sems.at[n]))
        for load in loads:
            load.start()
        for load in loads:
            load.wait()
        for r in range(0, rows, 128):
            out_ref[r : r + 128, :] = jnp.dot(
                at[:, r : r + 128].T, w_ref[...], preferred_element_type=F32
            ).astype(BF16)

    return pl.pallas_call(
        body,
        out_shape=jax.ShapeDtypeStruct((rows, D), BF16),
        in_specs=[SMEM] + [ANY] * (heads_dev * seq_size) + [VMEM],
        out_specs=VMEM,
        scratch_shapes=[
            pltpu.VMEM((HEADS * HD, rows), BF16),
            pltpu.SemaphoreType.DMA((heads_dev * seq_size,)),
        ],
        compiler_params=params(),
        cost_estimate=cost(2 * rows * D * D, 2 * D * D + 4 * rows * D),
        name="project_out",
    )(meta, *[x for head in pieces for x in head], w_out)


def shifted(x, axis, size, shift):
    return lax.ppermute(x, axis, [(i, (i + shift) % size) for i in range(size)])


def crossed(x, size, k):
    return lax.ppermute(x, "seq", [(i, i ^ k) for i in range(size)])


def on_device(nodes, w_qkv, w_out, kv_ids, counts):
    seq_size = lax.axis_size("seq")
    ncl = lax.axis_size("cluster")
    heads_dev = HEADS // seq_size
    npair = seq_size // 2
    nblk = seq_size * nodes.shape[0] // BLK
    cap = nblk // 4
    seq = lax.axis_index("seq")
    cluster = lax.axis_index("cluster")
    meta = jnp.stack([seq // 2, seq % 2, cluster, seq]).astype(jnp.int32)

    other = crossed(nodes, seq_size, 1)

    near_ids = (kv_ids[:, :NEAR] - cluster * nblk).reshape(-1)
    remote_ids = kv_ids[:, NEAR:]
    valid = jnp.arange(NEAR, KVB, dtype=jnp.int32)[None, :] < counts[:, None]
    every = jnp.arange(ncl * nblk, dtype=jnp.int32)
    present = jnp.any(
        (remote_ids.reshape(-1)[:, None] == every[None, :]) & valid.reshape(-1)[:, None], axis=0
    )
    present = present.astype(jnp.int32).reshape(ncl, nblk)
    rank = jnp.cumsum(present, axis=1) - 1
    chosen = (rank[:, None, :] == jnp.arange(cap, dtype=jnp.int32)[None, :, None]) & (
        present[:, None, :] > 0
    )
    wanted = jnp.sum(jnp.where(chosen, jnp.arange(nblk, dtype=jnp.int32)[None, None, :], 0), axis=2)
    asked = lax.all_to_all(wanted, "cluster", split_axis=0, concat_axis=0, tiled=True).reshape(-1)
    place = (remote_ids // nblk) * cap + jnp.sum(
        jnp.where(remote_ids[:, :, None] == every[None, None, :], rank.reshape(-1)[None, None, :], 0),
        axis=2,
    )
    pos = jnp.where(valid, place, place[:, :1]).reshape(-1)

    spans = [[((3 * h + 1) * HD, 2 * HD)] for h in range(heads_dev)]
    q_span = [(3 * h * HD, HD) for h in range(heads_dev)]
    (kv_first,) = project(spans[:1], heads_dev, npair, meta, nodes, other, w_qkv)
    rest = project(spans[1:] + [q_span], heads_dev, npair, meta, nodes, other, w_qkv)
    kinds = [kv_first] + rest
    arrived = [
        [x if j == 0 else crossed(x, seq_size, 2 * j) for j, x in enumerate(kind)] for kind in kinds
    ]
    kvs, queries = arrived[:heads_dev], arrived[heads_dev]
    far = []
    for h in range(heads_dev):
        picked = select(npair, ncl, cap, meta, asked, kvs[h])
        far.append([shifted(x, "cluster", ncl, s + 1) for s, x in enumerate(picked)])
    near, stats = near_attention(
        heads_dev, npair, meta, near_ids, [x for kv in kvs for x in kv], queries
    )
    pieces = []
    for h in range(heads_dev):
        outs = far_attention(
            h, heads_dev, npair, seq_size, ncl, cap, meta, pos, counts, far[h], queries, near, stats
        )
        pieces.append([x if k == 0 else crossed(x, seq_size, k) for k, x in enumerate(outs)])
    return project_out(heads_dev, seq_size, meta, pieces, w_out)


def solution(mesh):
    placed = (P(("cluster", "seq"), None), P(), P(), P("cluster", None), P("cluster"))
    return jax.shard_map(
        on_device,
        mesh=mesh,
        in_specs=placed,
        out_specs=P(("cluster", "seq"), None),
        check_vma=False,
    )
```

```python
import jax
import jax.numpy as jnp
from jax import lax
from jax.experimental import pallas as pl
from jax.experimental.pallas import tpu as pltpu
from jax.sharding import PartitionSpec as P

D = 1024
HEADS = 16
HD = 64
BLK = 128
KVB = 16
REMOTE = 4
NEAR = KVB - REMOTE
LOG2E = 1.4426950408889634
F32 = jnp.float32
BF16 = jnp.bfloat16

ANY = pl.BlockSpec(memory_space=pl.ANY)
SMEM = pl.BlockSpec(memory_space=pltpu.SMEM)
VMEM = pl.BlockSpec(memory_space=pltpu.VMEM)


def params(mib):
    return pltpu.CompilerParams(vmem_limit_bytes=mib * 1024 * 1024)


def cost(flops, byts, trans=0):
    return pl.CostEstimate(flops=flops, bytes_accessed=byts, transcendentals=trans)


def nt_dot(a, b):
    return lax.dot_general(a, b, (((1,), (1,)), ((), ())), preferred_element_type=F32)


def project(parts, heads_dev, npair, meta, own, other, w_qkv):
    rows = own.shape[0]
    group = 3 * HD * heads_dev
    shared = group % 128 != 0
    slab = 2 * group if shared else group
    top = slab if shared else max(s + n for part in parts for s, n in part)
    width = -(-top // 128) * 128
    heights = [sum(n for _, n in part) for part in parts]
    total = sum(heights)

    def body(meta_ref, own_ref, other_ref, w_ref, *refs):
        outs = refs[: len(parts) * npair]
        x, w, wt, turned, sems = refs[len(parts) * npair :]
        pair = meta_ref[0]
        core = meta_ref[1]
        loads = []
        for j in range(npair):
            dest = pair ^ j
            start = dest * slab if shared else (2 * dest + core) * slab
            loads.append(
                pltpu.make_async_copy(
                    w_ref.at[:, pl.ds(pl.multiple_of(start, 128), width)], w.at[j], sems.at[j]
                )
            )
        here = pl.multiple_of(core * rows, 128)
        there = pl.multiple_of((1 - core) * rows, 128)
        loads.append(pltpu.make_async_copy(own_ref, x.at[pl.ds(here, rows)], sems.at[npair]))
        loads.append(pltpu.make_async_copy(other_ref, x.at[pl.ds(there, rows)], sems.at[npair + 1]))
        for load in loads:
            load.start()
        for j in range(npair):
            loads[j].wait()
            if shared:
                turned[...] = w[j].T
            else:
                full = w[j].T
            at = j * total
            for part in parts:
                for s, n in part:
                    if shared:
                        off = pl.multiple_of(core * group + s, HD)
                        wt[at : at + n, :] = turned[pl.ds(off, n), :]
                    else:
                        wt[at : at + n, :] = full[s : s + n, :]
                    at += n
        loads[npair].wait()
        loads[npair + 1].wait()
        step = 256
        for r in range(0, 2 * rows, step):
            res = nt_dot(wt[...], x[r : r + step, :]).astype(BF16)
            for j in range(npair):
                at = j * total
                for k in range(len(parts)):
                    outs[k * npair + j][:, r : r + step] = res[at : at + heights[k], :]
                    at += heights[k]

    shapes = [jax.ShapeDtypeStruct((heights[k], 2 * rows), BF16) for k in range(len(parts)) for _ in range(npair)]
    outs = pl.pallas_call(
        body,
        out_shape=shapes,
        in_specs=[SMEM, ANY, ANY, ANY],
        out_specs=[VMEM] * len(shapes),
        scratch_shapes=[
            pltpu.VMEM((2 * rows, D), BF16),
            pltpu.VMEM((npair, D, width), BF16),
            pltpu.VMEM((npair * total, D), BF16),
            pltpu.VMEM((width, D) if shared else (16, 128), BF16),
            pltpu.SemaphoreType.DMA((npair + 2,)),
        ],
        compiler_params=params(60),
        cost_estimate=cost(2 * 2 * rows * D * total * npair, 4 * rows * D + 2 * D * width * npair),
        name="project",
    )(meta, own, other, w_qkv)
    return [list(outs[k * npair : (k + 1) * npair]) for k in range(len(parts))]


def select(npair, ncl, cap, meta, asked, tables, row):
    wide = tables[0].shape[1]
    per = wide // BLK

    def body(meta_ref, asked_ref, *refs):
        tabs = refs[:npair]
        outs = refs[npair : npair + ncl - 1]
        held, in_sems, out_sems = refs[npair + ncl - 1 :]
        pair = meta_ref[0]
        cluster = meta_ref[2]
        loads = [
            pltpu.make_async_copy(tabs[j].at[pl.ds(row, 2 * HD)], held.at[pair ^ j], in_sems.at[j])
            for j in range(npair)
        ]
        for load in loads:
            load.start()
        for load in loads:
            load.wait()
        sends = []
        for s in range(1, ncl):
            dest = lax.rem(cluster + s, ncl)
            for i in range(cap):
                block = asked_ref[dest, 0, i]
                lane = pl.multiple_of(lax.rem(block, per) * BLK, BLK)
                sends.append(
                    pltpu.make_async_copy(
                        held.at[block // per, :, pl.ds(lane, BLK)],
                        outs[s - 1].at[i],
                        out_sems.at[(s - 1) * cap + i],
                    )
                )
        for send in sends:
            send.start()
        for send in sends:
            send.wait()

    shape = jax.ShapeDtypeStruct((cap, 2 * HD, BLK), BF16)
    return pl.pallas_call(
        body,
        out_shape=[shape] * (ncl - 1),
        in_specs=[SMEM, SMEM] + [ANY] * npair,
        out_specs=[ANY] * (ncl - 1),
        scratch_shapes=[
            pltpu.VMEM((npair, 2 * HD, wide), BF16),
            pltpu.SemaphoreType.DMA((npair,)),
            pltpu.SemaphoreType.DMA(((ncl - 1) * cap,)),
        ],
        compiler_params=params(40),
        cost_estimate=cost(0, 4 * npair * 2 * HD * wide),
        name="select",
    )(meta, asked, *tables)


def query_matrix(heads_dev, q, per, b):
    lane = pl.multiple_of(lax.rem(b, per) * BLK, BLK)
    x = q[b // per, :, pl.ds(lane, BLK)] * jnp.asarray(HD**-0.5, BF16)
    zero = jnp.zeros((HD, BLK), BF16)
    if heads_dev == 1:
        return jnp.concatenate([x, zero], axis=0)
    left = jnp.concatenate([x[:HD], zero], axis=0)
    right = jnp.concatenate([zero, x[HD:]], axis=0)
    return jnp.concatenate([left, right], axis=1)


def near_attention(heads_dev, npair, meta, ids, first_kv, rest):
    wide = rest[0].shape[1]
    per = wide // BLK
    nblk = npair * per
    feats = heads_dev * HD
    low_q = (heads_dev - 1) * 2 * HD
    cols = heads_dev * BLK
    keys = NEAR * BLK

    def body(meta_ref, ids_ref, *refs):
        tabs = refs[:npair]
        rests = refs[npair : 2 * npair]
        out_ref, stat_ref, kv, q, ktab, vtab, s_a, s_b, sems = refs[2 * npair :]
        pair = meta_ref[0]
        loads = []
        for j in range(npair):
            at = pair ^ j
            loads.append(pltpu.make_async_copy(tabs[j], kv.at[0, at], sems.at[j]))
            for h in range(1, heads_dev):
                loads.append(
                    pltpu.make_async_copy(
                        rests[j].at[pl.ds((h - 1) * 2 * HD, 2 * HD)], kv.at[h, at], sems.at[h * npair + j]
                    )
                )
            loads.append(
                pltpu.make_async_copy(
                    rests[j].at[pl.ds(low_q, feats)], q.at[at], sems.at[heads_dev * npair + j]
                )
            )
        for load in loads:
            load.start()
        for load in loads:
            load.wait()

        def build(p, carry):
            for i in range(per):
                at = slice(i * BLK, (i + 1) * BLK)
                pieces = [kv[h, p, :, at] for h in range(heads_dev)]
                if heads_dev == 1:
                    ktab[p * per + i] = pieces[0].T
                else:
                    ktab[p * per + i] = jnp.concatenate([x[:HD] for x in pieces], axis=0).T
                vtab[p * per + i] = jnp.concatenate([x[HD:] for x in pieces], axis=0)
            return carry

        lax.fori_loop(0, npair, build, 0)

        def first(b, held):
            qm = query_matrix(heads_dev, q, per, b)
            top = None
            for j in range(NEAR):
                s = jnp.dot(ktab[ids_ref[b * NEAR + j]], qm, preferred_element_type=F32)
                held[j * BLK : (j + 1) * BLK, :] = s
                part = jnp.max(s.reshape(BLK // 8, 8, cols), axis=0)
                top = part if top is None else jnp.maximum(top, part)
            return jnp.max(top, axis=0, keepdims=True)

        def second(b, held, top):
            acc = None
            total = None
            for c in range(0, NEAR, 4):
                p = jnp.exp2((held[c * BLK : (c + 4) * BLK, :] - top) * LOG2E)
                part = jnp.sum(p.reshape(4 * BLK // 8, 8, cols), axis=0)
                total = part if total is None else total + part
                v = jnp.concatenate([vtab[ids_ref[b * NEAR + c + i]] for i in range(4)], axis=1)
                o = jnp.dot(v, p.astype(BF16), preferred_element_type=F32)
                acc = o if acc is None else acc + o
            out_ref[b] = jnp.concatenate(
                [
                    acc[h * HD : (h + 1) * HD, h * BLK : (h + 1) * BLK]
                    for h in range(heads_dev)
                ],
                axis=0,
            )
            stat_ref[b, 0:1, :] = top
            stat_ref[b, 1:2, :] = jnp.sum(total, axis=0, keepdims=True)

        def step(i, top):
            b = 2 * i
            top_b = first(b + 1, s_b)
            second(b, s_a, top)
            top_a = first(jnp.minimum(b + 2, nblk - 1), s_a)
            second(b + 1, s_b, top_b)
            return top_a

        lax.fori_loop(0, nblk // 2, step, first(0, s_a))

    flops = nblk * keys * BLK * feats * 4 * heads_dev
    return pl.pallas_call(
        body,
        out_shape=[
            jax.ShapeDtypeStruct((nblk, feats, BLK), F32),
            jax.ShapeDtypeStruct((nblk, 8, cols), F32),
        ],
        in_specs=[SMEM, SMEM] + [ANY] * (2 * npair),
        out_specs=[VMEM, VMEM],
        scratch_shapes=[
            pltpu.VMEM((heads_dev, npair, 2 * HD, wide), BF16),
            pltpu.VMEM((npair, feats, wide), BF16),
            pltpu.VMEM((nblk, BLK, 2 * HD), BF16),
            pltpu.VMEM((nblk, feats, BLK), BF16),
            pltpu.VMEM((keys, cols), F32),
            pltpu.VMEM((keys, cols), F32),
            pltpu.SemaphoreType.DMA((npair * (heads_dev + 1),)),
        ],
        compiler_params=params(40),
        cost_estimate=cost(2 * flops, 8 * nblk * BLK * feats, nblk * keys * cols),
        name="near_attention",
    )(meta, ids, *first_kv, *rest)


def far_attention(heads_dev, npair, seq_size, ncl, cap, meta, pos, counts, tables, rest, near, stats):
    wide = rest[0].shape[1]
    per = wide // BLK
    nblk = npair * per
    low_q = (heads_dev - 1) * 2 * HD
    dev_blocks = nblk // seq_size
    feats = heads_dev * HD
    cols = heads_dev * BLK
    keys = REMOTE * BLK
    shifts = ncl - 1

    def body(meta_ref, pos_ref, counts_ref, *refs):
        tabs = refs[: heads_dev * shifts]
        refs = refs[heads_dev * shifts :]
        rests = refs[:npair]
        near_ref, stat_ref = refs[npair : npair + 2]
        outs = refs[npair + 2 : npair + 2 + seq_size]
        kv, q, ktab, vtab, old, s_a, s_b, sems = refs[npair + 2 + seq_size :]
        pair = meta_ref[0]
        cluster = meta_ref[2]
        seq = meta_ref[3]
        loads = []
        for h in range(heads_dev):
            for s in range(shifts):
                origin = lax.rem(cluster + ncl - 1 - s, ncl) * cap
                n = h * shifts + s
                loads.append(pltpu.make_async_copy(tabs[n], kv.at[h, pl.ds(origin, cap)], sems.at[n]))
        for j in range(npair):
            loads.append(
                pltpu.make_async_copy(
                    rests[j].at[pl.ds(low_q, feats)], q.at[pair ^ j], sems.at[heads_dev * shifts + j]
                )
            )
        late = []
        for k in range(seq_size):
            at = pl.ds((seq ^ k) * dev_blocks, dev_blocks)
            late.append(
                pltpu.make_async_copy(near_ref.at[at], old.at[at], sems.at[heads_dev * shifts + npair + k])
            )
        for load in loads + late:
            load.start()
        for load in loads:
            load.wait()

        def build(s, carry):
            origin = lax.rem(cluster + ncl - s, ncl) * cap
            for i in range(cap):
                pieces = [kv[h, origin + i] for h in range(heads_dev)]
                if heads_dev == 1:
                    ktab[origin + i] = pieces[0].T
                else:
                    ktab[origin + i] = jnp.concatenate([x[:HD] for x in pieces], axis=0).T
                vtab[origin + i] = jnp.concatenate([x[HD:] for x in pieces], axis=0)
            return carry

        lax.fori_loop(1, ncl, build, 0)

        def first(b, held):
            qm = query_matrix(heads_dev, q, per, b)
            valid = counts_ref[b] - NEAR
            top = None
            for j in range(REMOTE):
                s = jnp.dot(ktab[pos_ref[b * REMOTE + j]], qm, preferred_element_type=F32)
                if j:
                    s = jnp.where(j < valid, s, -1e30)
                held[j * BLK : (j + 1) * BLK, :] = s
                part = jnp.max(s.reshape(BLK // 8, 8, cols), axis=0)
                top = part if top is None else jnp.maximum(top, part)
            return jnp.max(top, axis=0, keepdims=True)

        def second(b, held, top):
            was = stat_ref[b, 0:1, :]
            top = jnp.maximum(was, top)
            fade = jnp.exp2((was - top) * LOG2E)
            p = jnp.exp2((held[...] - top) * LOG2E)
            part = jnp.sum(p.reshape(keys // 8, 8, cols), axis=0)
            total = stat_ref[b, 1:2, :] * fade + jnp.sum(part, axis=0, keepdims=True)
            v = jnp.concatenate([vtab[pos_ref[b * REMOTE + j]] for j in range(REMOTE)], axis=1)
            acc = jnp.dot(v, p.astype(BF16), preferred_element_type=F32)
            inv = 1.0 / total
            kept = fade * inv
            res = []
            for h in range(heads_dev):
                at, lane = slice(h * HD, (h + 1) * HD), slice(h * BLK, (h + 1) * BLK)
                res.append(acc[at, lane] * inv[:, lane] + old[b, at, :] * kept[:, lane])
            return jnp.concatenate(res, axis=0).astype(BF16)

        steps = [(k, i) for k in range(seq_size) for i in range(dev_blocks)]
        starts = [(seq ^ k) * dev_blocks + i for k, i in steps]
        helds = (s_a, s_b)
        top = first(starts[0], s_a)
        for n, (k, i) in enumerate(steps):
            if i == 0:
                late[k].wait()
            ahead = first(starts[n + 1], helds[(n + 1) % 2]) if n + 1 < len(steps) else None
            outs[k][:, i * BLK : (i + 1) * BLK] = second(starts[n], helds[n % 2], top)
            top = ahead

    flops = nblk * keys * BLK * feats * 4 * heads_dev
    return pl.pallas_call(
        body,
        out_shape=[jax.ShapeDtypeStruct((feats, dev_blocks * BLK), BF16)] * seq_size,
        in_specs=[SMEM, SMEM, SMEM] + [ANY] * (heads_dev * shifts + npair) + [ANY, VMEM],
        out_specs=[VMEM] * seq_size,
        scratch_shapes=[
            pltpu.VMEM((heads_dev, ncl * cap, 2 * HD, BLK), BF16),
            pltpu.VMEM((npair, feats, wide), BF16),
            pltpu.VMEM((ncl * cap, BLK, 2 * HD), BF16),
            pltpu.VMEM((ncl * cap, feats, BLK), BF16),
            pltpu.VMEM((nblk, feats, BLK), F32),
            pltpu.VMEM((keys, cols), F32),
            pltpu.VMEM((keys, cols), F32),
            pltpu.SemaphoreType.DMA((heads_dev * shifts + npair + seq_size,)),
        ],
        compiler_params=params(40),
        cost_estimate=cost(flops, 6 * nblk * BLK * feats, nblk * keys * cols),
        name="far_attention",
    )(meta, pos, counts, *[x for t in tables for x in t], *rest, near, stats)


def project_out(seq_size, meta, pieces, w_out):
    feats, rows = pieces[0].shape
    step = 128

    def body(meta_ref, *refs):
        parts = refs[:seq_size]
        w_ref, out_ref, at, out, sems = refs[seq_size:]
        seq = meta_ref[3]
        loads = []
        for k in range(seq_size):
            row = pl.multiple_of((seq ^ k) * feats, feats)
            loads.append(pltpu.make_async_copy(parts[k], at.at[pl.ds(row, feats)], sems.at[k]))
        for load in loads:
            load.start()
        for load in loads:
            load.wait()
        stores = []
        for n, r in enumerate(range(0, rows, step)):
            out[r : r + step, :] = jnp.dot(
                at[:, r : r + step].T, w_ref[...], preferred_element_type=F32
            ).astype(BF16)
            rows_at = pl.ds(r, step)
            stores.append(pltpu.make_async_copy(out.at[rows_at], out_ref.at[rows_at], sems.at[seq_size + n]))
            stores[-1].start()
        for store in stores:
            store.wait()

    return pl.pallas_call(
        body,
        out_shape=jax.ShapeDtypeStruct((rows, D), BF16),
        in_specs=[SMEM] + [ANY] * seq_size + [VMEM],
        out_specs=ANY,
        scratch_shapes=[
            pltpu.VMEM((HEADS * HD, rows), BF16),
            pltpu.VMEM((rows, D), BF16),
            pltpu.SemaphoreType.DMA((seq_size + rows // step,)),
        ],
        compiler_params=params(40),
        cost_estimate=cost(2 * rows * D * D, 2 * D * D + 4 * rows * D),
        name="project_out",
    )(meta, *pieces, w_out)


def shifted(x, axis, size, shift):
    return lax.ppermute(x, axis, [(i, (i + shift) % size) for i in range(size)])


def crossed(x, size, k):
    return lax.ppermute(x, "seq", [(i, i ^ k) for i in range(size)])


def wanted_blocks(kv_ids, counts, ncl, nblk):
    cap = nblk // 4
    remote_ids = kv_ids[:, NEAR:]
    valid = jnp.arange(NEAR, KVB, dtype=jnp.int32)[None, :] < counts[:, None]
    every = jnp.arange(ncl * nblk, dtype=jnp.int32)
    present = jnp.any(
        (remote_ids.reshape(-1)[:, None] == every[None, :]) & valid.reshape(-1)[:, None], axis=0
    )
    present = present.astype(jnp.int32).reshape(ncl, nblk)
    rank = jnp.cumsum(present, axis=1) - 1
    chosen = (rank[:, None, :] == jnp.arange(cap, dtype=jnp.int32)[None, :, None]) & (
        present[:, None, :] > 0
    )
    wanted = jnp.sum(jnp.where(chosen, jnp.arange(nblk, dtype=jnp.int32)[None, None, :], 0), axis=2)
    place = (remote_ids // nblk) * cap + jnp.sum(
        jnp.where(remote_ids[:, :, None] == every[None, None, :], rank.reshape(-1)[None, None, :], 0),
        axis=2,
    )
    return jnp.pad(wanted[:, None, :], ((0, 0), (0, 7), (0, 128 - cap))), jnp.where(valid, place, place[:, :1]).reshape(-1)


def on_device(nodes, w_qkv, w_out, kv_ids, counts):
    seq_size = lax.axis_size("seq")
    ncl = lax.axis_size("cluster")
    heads_dev = HEADS // seq_size
    npair = seq_size // 2
    nblk = seq_size * nodes.shape[0] // BLK
    cap = nblk // 4
    seq = lax.axis_index("seq")
    cluster = lax.axis_index("cluster")
    meta = jnp.stack([seq // 2, seq % 2, cluster, seq]).astype(jnp.int32)

    other = crossed(nodes, seq_size, 1)
    wanted, pos = wanted_blocks(kv_ids, counts, ncl, nblk)
    wanted, own = lax.optimization_barrier((wanted, nodes))

    q_span = [(3 * h * HD, HD) for h in range(heads_dev)]
    spans = [[((3 * h + 1) * HD, 2 * HD)] for h in range(heads_dev)]
    (first_kv,) = project(spans[:1], heads_dev, npair, meta, own, other, w_qkv)
    (rest,) = project([sum(spans[1:] + [q_span], [])], heads_dev, npair, meta, nodes, other, w_qkv)
    wanted, rest = lax.optimization_barrier((wanted, rest))
    asked = lax.all_to_all(wanted, "cluster", split_axis=0, concat_axis=0, tiled=True)
    first_kv = [x if j == 0 else crossed(x, seq_size, 2 * j) for j, x in enumerate(first_kv)]
    rest = [x if j == 0 else crossed(x, seq_size, 2 * j) for j, x in enumerate(rest)]
    far = []
    for h in range(heads_dev):
        tables, row = (first_kv, 0) if h == 0 else (rest, (h - 1) * 2 * HD)
        picked = select(npair, ncl, cap, meta, asked, tables, row)
        far.append([shifted(x, "cluster", ncl, s + 1) for s, x in enumerate(picked)])
    near_ids = (kv_ids[:, :NEAR] - cluster * nblk).reshape(-1)
    near, stats = near_attention(heads_dev, npair, meta, near_ids, first_kv, rest)
    outs = far_attention(
        heads_dev, npair, seq_size, ncl, cap, meta, pos, counts, far, rest, near, stats
    )
    pieces = [x if k == 0 else crossed(x, seq_size, k) for k, x in enumerate(outs)]
    return project_out(seq_size, meta, pieces, w_out)


def solution(mesh):
    placed = (P(("cluster", "seq"), None), P(), P(), P("cluster", None), P("cluster"))
    return jax.shard_map(
        on_device,
        mesh=mesh,
        in_specs=placed,
        out_specs=P(("cluster", "seq"), None),
        check_vma=False,
    )
```

```python
import jax
import jax.numpy as jnp
from jax import lax
from jax.experimental import pallas as pl
from jax.experimental.pallas import tpu as pltpu
from jax.sharding import PartitionSpec as P

D = 1024
HEADS = 16
HD = 64
BLK = 128
KVB = 16
REMOTE = 4
NEAR = KVB - REMOTE
NEAR_UNROLL = 4
FAR_UNROLL = 8
LOG2E = 1.4426950408889634
F32 = jnp.float32
BF16 = jnp.bfloat16

ANY = pl.BlockSpec(memory_space=pl.ANY)
SMEM = pl.BlockSpec(memory_space=pltpu.SMEM)
VMEM = pl.BlockSpec(memory_space=pltpu.VMEM)


def params(mib):
    return pltpu.CompilerParams(vmem_limit_bytes=mib * 1024 * 1024)


def cost(flops, byts, trans=0):
    return pl.CostEstimate(flops=flops, bytes_accessed=byts, transcendentals=trans)


def nt_dot(a, b):
    return lax.dot_general(a, b, (((1,), (1,)), ((), ())), preferred_element_type=F32)


def project(parts, heads_dev, npair, meta, own, other, w_qkv):
    rows = own.shape[0]
    group = 3 * HD * heads_dev
    shared = group % 128 != 0
    slab = 2 * group if shared else group
    top = slab if shared else max(s + n for part in parts for s, n in part)
    width = -(-top // 128) * 128
    heights = [sum(n for _, n in part) for part in parts]
    total = sum(heights)

    def body(meta_ref, own_ref, other_ref, w_ref, *refs):
        outs = refs[: len(parts) * npair]
        x, w, wt, turned, made, sems = refs[len(parts) * npair :]
        pair = meta_ref[0]
        core = meta_ref[1]
        loads = []
        for j in range(npair):
            dest = pair ^ j
            start = dest * slab if shared else (2 * dest + core) * slab
            loads.append(
                pltpu.make_async_copy(
                    w_ref.at[:, pl.ds(pl.multiple_of(start, 128), width)], w.at[j], sems.at[j]
                )
            )
        here = pl.multiple_of(core * rows, 128)
        there = pl.multiple_of((1 - core) * rows, 128)
        loads.append(pltpu.make_async_copy(own_ref, x.at[pl.ds(here, rows)], sems.at[npair]))
        loads.append(pltpu.make_async_copy(other_ref, x.at[pl.ds(there, rows)], sems.at[npair + 1]))
        for load in loads:
            load.start()
        for j in range(npair):
            loads[j].wait()
            if shared:
                turned[...] = w[j].T
            else:
                full = w[j].T
            at = j * total
            for part in parts:
                for s, n in part:
                    if shared:
                        off = pl.multiple_of(core * group + s, HD)
                        wt[at : at + n, :] = turned[pl.ds(off, n), :]
                    else:
                        wt[at : at + n, :] = full[s : s + n, :]
                    at += n
        step = 256
        stores = []
        for half in range(2):
            loads[npair + half].wait()
            for r in range(0, rows, step):
                at_rows = pl.multiple_of((here if half == 0 else there) + r, step)
                res = nt_dot(wt[...], x[pl.ds(at_rows, step), :]).astype(BF16)
                made[:, half * rows + r : half * rows + r + step] = res
                for j in range(npair):
                    at = j * total
                    for k in range(len(parts)):
                        stores.append(
                            pltpu.make_async_copy(
                                made.at[at : at + heights[k], half * rows + r : half * rows + r + step],
                                outs[k * npair + j].at[:, pl.ds(at_rows, step)],
                                sems.at[npair + 2 + len(stores)],
                            )
                        )
                        stores[-1].start()
                        at += heights[k]
        for store in stores:
            store.wait()

    shapes = [jax.ShapeDtypeStruct((heights[k], 2 * rows), BF16) for k in range(len(parts)) for _ in range(npair)]
    outs = pl.pallas_call(
        body,
        out_shape=shapes,
        in_specs=[SMEM, ANY, ANY, ANY],
        out_specs=[ANY] * len(shapes),
        scratch_shapes=[
            pltpu.VMEM((2 * rows, D), BF16),
            pltpu.VMEM((npair, D, width), BF16),
            pltpu.VMEM((npair * total, D), BF16),
            pltpu.VMEM((width, D) if shared else (16, 128), BF16),
            pltpu.VMEM((npair * total, 2 * rows), BF16),
            pltpu.SemaphoreType.DMA((npair + 2 + npair * len(parts) * 2 * rows // 256,)),
        ],
        compiler_params=params(55),
        cost_estimate=cost(2 * 2 * rows * D * total * npair, 4 * rows * D + 2 * D * width * npair),
        name="project",
    )(meta, own, other, w_qkv)
    return [list(outs[k * npair : (k + 1) * npair]) for k in range(len(parts))]


def select(npair, ncl, cap, meta, asked, tables, row):
    wide = tables[0].shape[1]
    per = wide // BLK

    def body(meta_ref, asked_ref, *refs):
        tabs = refs[:npair]
        outs = refs[npair : npair + ncl - 1]
        held, in_sems, out_sems = refs[npair + ncl - 1 :]
        pair = meta_ref[0]
        cluster = meta_ref[2]
        loads = [
            pltpu.make_async_copy(tabs[j].at[pl.ds(row, 2 * HD)], held.at[pair ^ j], in_sems.at[j])
            for j in range(npair)
        ]
        for load in loads:
            load.start()
        for load in loads:
            load.wait()
        sends = []
        for s in range(1, ncl):
            for i in range(cap):
                block = asked_ref[lax.rem(cluster + s, ncl), 0, i]
                lane = pl.multiple_of(lax.rem(block, per) * BLK, BLK)
                sends.append(
                    pltpu.make_async_copy(
                        held.at[block // per, :, pl.ds(lane, BLK)],
                        outs[s - 1].at[i],
                        out_sems.at[(s - 1) * cap + i],
                    )
                )
        for send in sends:
            send.start()
        for send in sends:
            send.wait()

    shape = jax.ShapeDtypeStruct((cap, 2 * HD, BLK), BF16)
    return pl.pallas_call(
        body,
        out_shape=[shape] * (ncl - 1),
        in_specs=[SMEM, SMEM] + [ANY] * npair,
        out_specs=[ANY] * (ncl - 1),
        scratch_shapes=[
            pltpu.VMEM((npair, 2 * HD, wide), BF16),
            pltpu.SemaphoreType.DMA((npair,)),
            pltpu.SemaphoreType.DMA(((ncl - 1) * cap,)),
        ],
        compiler_params=params(40),
        cost_estimate=cost(0, 4 * npair * 2 * HD * wide),
        name="select",
    )(meta, asked, *tables)


def query_matrix(heads_dev, q, per, b):
    lane = pl.multiple_of(lax.rem(b, per) * BLK, BLK)
    x = q[b // per, :, pl.ds(lane, BLK)] * jnp.asarray(HD**-0.5, BF16)
    zero = jnp.zeros((HD, BLK), BF16)
    if heads_dev == 1:
        return jnp.concatenate([x, zero], axis=0)
    left = jnp.concatenate([x[:HD], zero], axis=0)
    right = jnp.concatenate([zero, x[HD:]], axis=0)
    return jnp.concatenate([left, right], axis=1)


def near_attention(heads_dev, npair, meta, ids, first_kv, rest):
    wide = rest[0].shape[1]
    per = wide // BLK
    nblk = npair * per
    feats = heads_dev * HD
    low_q = (heads_dev - 1) * 2 * HD
    cols = heads_dev * BLK
    keys = NEAR * BLK

    def body(meta_ref, ids_ref, *refs):
        tabs = refs[:npair]
        rests = refs[npair : 2 * npair]
        out_ref, stat_ref, kv, q, ktab, vtab, s_a, s_b, t_a, t_b, sems = refs[2 * npair :]
        pair = meta_ref[0]
        base = meta_ref[2] * nblk
        loads = []
        for j in range(npair):
            at = pair ^ j
            loads.append(pltpu.make_async_copy(tabs[j], kv.at[0, at], sems.at[j]))
            for h in range(1, heads_dev):
                loads.append(
                    pltpu.make_async_copy(
                        rests[j].at[pl.ds((h - 1) * 2 * HD, 2 * HD)], kv.at[h, at], sems.at[h * npair + j]
                    )
                )
            loads.append(
                pltpu.make_async_copy(
                    rests[j].at[pl.ds(low_q, feats)], q.at[at], sems.at[heads_dev * npair + j]
                )
            )
        for load in loads:
            load.start()
        for load in loads:
            load.wait()

        def build(p, carry):
            for i in range(per):
                at = slice(i * BLK, (i + 1) * BLK)
                pieces = [kv[h, p, :, at] for h in range(heads_dev)]
                if heads_dev == 1:
                    ktab[p * per + i] = pieces[0].T
                else:
                    ktab[p * per + i] = jnp.concatenate([x[:HD] for x in pieces], axis=0).T
                vtab[p * per + i] = jnp.concatenate([x[HD:] for x in pieces], axis=0)
            return carry

        lax.fori_loop(0, npair, build, 0)

        def scores(b, qm, held, c, best):
            for j in range(c, c + 4):
                s = jnp.dot(ktab[ids_ref[j, b] - base], qm, preferred_element_type=F32)
                held[j * BLK : (j + 1) * BLK, :] = s
                part = jnp.max(s.reshape(BLK // 8, 8, cols), axis=0)
                best = part if best is None else jnp.maximum(best, part)
            return best

        def values(b, held, top, c, acc, total):
            p = jnp.exp2((held[c * BLK : (c + 4) * BLK, :] - top) * LOG2E)
            part = jnp.sum(p.reshape(4 * BLK // 8, 8, cols), axis=0)
            v = jnp.concatenate([vtab[ids_ref[c + i, b] - base] for i in range(4)], axis=1)
            o = jnp.dot(v, p.astype(BF16), preferred_element_type=F32)
            return (o, part) if acc is None else (acc + o, total + part)

        def stage(start, held, top_ref, held_after, top_after):
            for u in range(NEAR_UNROLL):
                b = start + u
                after = jnp.minimum(b + NEAR_UNROLL, nblk - 1)
                qm = query_matrix(heads_dev, q, per, after)
                top = top_ref[u]
                acc = total = best = None
                for c in range(0, NEAR, 4):
                    best = scores(after, qm, held_after.at[u], c, best)
                    acc, total = values(b, held.at[u], top, c, acc, total)
                top_after[u] = jnp.max(best, axis=0, keepdims=True)
                out_ref[b] = jnp.concatenate(
                    [acc[h * HD : (h + 1) * HD, h * BLK : (h + 1) * BLK] for h in range(heads_dev)],
                    axis=0,
                )
                stat_ref[b, 0:1, :] = top
                stat_ref[b, 1:2, :] = jnp.sum(total, axis=0, keepdims=True)

        for u in range(NEAR_UNROLL):
            qm = query_matrix(heads_dev, q, per, u)
            best = None
            for c in range(0, NEAR, 4):
                best = scores(u, qm, s_a.at[u], c, best)
            t_a[u] = jnp.max(best, axis=0, keepdims=True)

        def step(n, carry):
            b = n * NEAR_UNROLL
            pl.when(lax.rem(n, 2) == 0)(lambda: stage(b, s_a, t_a, s_b, t_b))
            pl.when(lax.rem(n, 2) == 1)(lambda: stage(b, s_b, t_b, s_a, t_a))
            return carry

        lax.fori_loop(0, nblk // NEAR_UNROLL, step, 0)

    flops = nblk * keys * BLK * feats * 4 * heads_dev
    return pl.pallas_call(
        body,
        out_shape=[
            jax.ShapeDtypeStruct((nblk, feats, BLK), F32),
            jax.ShapeDtypeStruct((nblk, 8, cols), F32),
        ],
        in_specs=[SMEM, SMEM] + [ANY] * (2 * npair),
        out_specs=[VMEM, VMEM],
        scratch_shapes=[
            pltpu.VMEM((heads_dev, npair, 2 * HD, wide), BF16),
            pltpu.VMEM((npair, feats, wide), BF16),
            pltpu.VMEM((nblk, BLK, 2 * HD), BF16),
            pltpu.VMEM((nblk, feats, BLK), BF16),
            pltpu.VMEM((NEAR_UNROLL, keys, cols), F32),
            pltpu.VMEM((NEAR_UNROLL, keys, cols), F32),
            pltpu.VMEM((NEAR_UNROLL, 1, cols), F32),
            pltpu.VMEM((NEAR_UNROLL, 1, cols), F32),
            pltpu.SemaphoreType.DMA((npair * (heads_dev + 1),)),
        ],
        compiler_params=params(40),
        cost_estimate=cost(2 * flops, 8 * nblk * BLK * feats, nblk * keys * cols),
        name="near_attention",
    )(meta, ids, *first_kv, *rest)


def far_attention(heads_dev, npair, seq_size, ncl, cap, meta, pos, counts, tables, rest, near, stats):
    wide = rest[0].shape[1]
    per = wide // BLK
    nblk = npair * per
    low_q = (heads_dev - 1) * 2 * HD
    dev_blocks = nblk // seq_size
    feats = heads_dev * HD
    cols = heads_dev * BLK
    keys = REMOTE * BLK
    shifts = ncl - 1

    def body(meta_ref, pos_ref, counts_ref, *refs):
        tabs = refs[: heads_dev * shifts]
        refs = refs[heads_dev * shifts :]
        rests = refs[:npair]
        near_ref, stat_ref = refs[npair : npair + 2]
        outs = refs[npair + 2 : npair + 2 + seq_size]
        kv, q, ktab, vtab, old, s_a, s_b, t_a, t_b, att, sems = refs[npair + 2 + seq_size :]
        pair = meta_ref[0]
        cluster = meta_ref[2]
        seq = meta_ref[3]
        loads = []
        for h in range(heads_dev):
            for s in range(shifts):
                origin = lax.rem(cluster + ncl - 1 - s, ncl) * cap
                n = h * shifts + s
                loads.append(pltpu.make_async_copy(tabs[n], kv.at[h, pl.ds(origin, cap)], sems.at[n]))
        for j in range(npair):
            loads.append(
                pltpu.make_async_copy(
                    rests[j].at[pl.ds(low_q, feats)], q.at[pair ^ j], sems.at[heads_dev * shifts + j]
                )
            )
        late = []
        for k in range(seq_size):
            at = pl.ds((seq ^ k) * dev_blocks, dev_blocks)
            late.append(
                pltpu.make_async_copy(near_ref.at[at], old.at[at], sems.at[heads_dev * shifts + npair + k])
            )
        for load in loads + late:
            load.start()
        for load in loads:
            load.wait()

        def build(s, carry):
            origin = lax.rem(cluster + ncl - s, ncl) * cap
            for i in range(cap):
                pieces = [kv[h, origin + i] for h in range(heads_dev)]
                if heads_dev == 1:
                    ktab[origin + i] = pieces[0].T
                else:
                    ktab[origin + i] = jnp.concatenate([x[:HD] for x in pieces], axis=0).T
                vtab[origin + i] = jnp.concatenate([x[HD:] for x in pieces], axis=0)
            return carry

        lax.fori_loop(1, ncl, build, 0)

        for load in late:
            load.wait()

        def block_of(n):
            return (seq ^ (n // dev_blocks)) * dev_blocks + lax.rem(n, dev_blocks)

        def scores(b, qm, held, c, best):
            valid = counts_ref[b] - NEAR
            for j in range(c, c + 4):
                s = jnp.dot(ktab[pos_ref[j, b]], qm, preferred_element_type=F32)
                if j:
                    s = jnp.where(j < valid, s, -1e30)
                held[j * BLK : (j + 1) * BLK, :] = s
                part = jnp.max(s.reshape(BLK // 8, 8, cols), axis=0)
                best = part if best is None else jnp.maximum(best, part)
            return best

        def values(b, held, top, c, acc, total):
            p = jnp.exp2((held[c * BLK : (c + 4) * BLK, :] - top) * LOG2E)
            part = jnp.sum(p.reshape(4 * BLK // 8, 8, cols), axis=0)
            v = jnp.concatenate([vtab[pos_ref[c + i, b]] for i in range(4)], axis=1)
            o = jnp.dot(v, p.astype(BF16), preferred_element_type=F32)
            return (o, part) if acc is None else (acc + o, total + part)

        def stage(start, held, top_ref, held_after, top_after):
            for u in range(FAR_UNROLL):
                n = start + u
                b = block_of(n)
                after = block_of(jnp.minimum(n + FAR_UNROLL, nblk - 1))
                qm = query_matrix(heads_dev, q, per, after)
                was = stat_ref[b, 0:1, :]
                top = jnp.maximum(was, top_ref[u])
                acc = total_f = best = None
                for c in range(0, REMOTE, 4):
                    best = scores(after, qm, held_after.at[u], c, best)
                    acc, total_f = values(b, held.at[u], top, c, acc, total_f)
                top_after[u] = jnp.max(best, axis=0, keepdims=True)
                fade = jnp.exp2((was - top) * LOG2E)
                inv = 1.0 / (stat_ref[b, 1:2, :] * fade + jnp.sum(total_f, axis=0, keepdims=True))
                kept = fade * inv
                res = []
                for h in range(heads_dev):
                    at, lane = slice(h * HD, (h + 1) * HD), slice(h * BLK, (h + 1) * BLK)
                    res.append(acc[at, lane] * inv[:, lane] + old[b, at, :] * kept[:, lane])
                att[n] = jnp.concatenate(res, axis=0).astype(BF16)

        for u in range(FAR_UNROLL):
            b = block_of(u)
            qm = query_matrix(heads_dev, q, per, b)
            best = None
            for c in range(0, REMOTE, 4):
                best = scores(b, qm, s_a.at[u], c, best)
            t_a[u] = jnp.max(best, axis=0, keepdims=True)

        def step(i, carry):
            n = i * FAR_UNROLL
            pl.when(lax.rem(i, 2) == 0)(lambda: stage(n, s_a, t_a, s_b, t_b))
            pl.when(lax.rem(i, 2) == 1)(lambda: stage(n, s_b, t_b, s_a, t_a))
            return carry

        lax.fori_loop(0, nblk // FAR_UNROLL, step, 0)
        for k in range(seq_size):
            for i in range(dev_blocks):
                outs[k][:, i * BLK : (i + 1) * BLK] = att[k * dev_blocks + i]

    flops = nblk * keys * BLK * feats * 4 * heads_dev
    return pl.pallas_call(
        body,
        out_shape=[jax.ShapeDtypeStruct((feats, dev_blocks * BLK), BF16)] * seq_size,
        in_specs=[SMEM, SMEM, SMEM] + [ANY] * (heads_dev * shifts + npair) + [ANY, VMEM],
        out_specs=[VMEM] * seq_size,
        scratch_shapes=[
            pltpu.VMEM((heads_dev, ncl * cap, 2 * HD, BLK), BF16),
            pltpu.VMEM((npair, feats, wide), BF16),
            pltpu.VMEM((ncl * cap, BLK, 2 * HD), BF16),
            pltpu.VMEM((ncl * cap, feats, BLK), BF16),
            pltpu.VMEM((nblk, feats, BLK), F32),
            pltpu.VMEM((FAR_UNROLL, keys, cols), F32),
            pltpu.VMEM((FAR_UNROLL, keys, cols), F32),
            pltpu.VMEM((FAR_UNROLL, 1, cols), F32),
            pltpu.VMEM((FAR_UNROLL, 1, cols), F32),
            pltpu.VMEM((nblk, feats, BLK), BF16),
            pltpu.SemaphoreType.DMA((heads_dev * shifts + npair + seq_size,)),
        ],
        compiler_params=params(40),
        cost_estimate=cost(flops, 6 * nblk * BLK * feats, nblk * keys * cols),
        name="far_attention",
    )(meta, pos, counts, *[x for t in tables for x in t], *rest, near, stats)


def project_out(seq_size, meta, pieces, w_out):
    feats, rows = pieces[0].shape
    step = 128

    def body(meta_ref, *refs):
        parts = refs[:seq_size]
        w_ref, out_ref, at, out, sems = refs[seq_size:]
        seq = meta_ref[3]
        loads = []
        for k in range(seq_size):
            row = pl.multiple_of((seq ^ k) * feats, feats)
            loads.append(pltpu.make_async_copy(parts[k], at.at[pl.ds(row, feats)], sems.at[k]))
        for load in loads:
            load.start()
        for load in loads:
            load.wait()
        stores = []
        for n, r in enumerate(range(0, rows, step)):
            out[r : r + step, :] = jnp.dot(
                at[:, r : r + step].T, w_ref[...], preferred_element_type=F32
            ).astype(BF16)
            rows_at = pl.ds(r, step)
            stores.append(pltpu.make_async_copy(out.at[rows_at], out_ref.at[rows_at], sems.at[seq_size + n]))
            stores[-1].start()
        for store in stores:
            store.wait()

    return pl.pallas_call(
        body,
        out_shape=jax.ShapeDtypeStruct((rows, D), BF16),
        in_specs=[SMEM] + [ANY] * seq_size + [VMEM],
        out_specs=ANY,
        scratch_shapes=[
            pltpu.VMEM((HEADS * HD, rows), BF16),
            pltpu.VMEM((rows, D), BF16),
            pltpu.SemaphoreType.DMA((seq_size + rows // step,)),
        ],
        compiler_params=params(40),
        cost_estimate=cost(2 * rows * D * D, 2 * D * D + 4 * rows * D),
        name="project_out",
    )(meta, *pieces, w_out)


def shifted(x, axis, size, shift):
    return lax.ppermute(x, axis, [(i, (i + shift) % size) for i in range(size)])


def crossed(x, size, k):
    return lax.ppermute(x, "seq", [(i, i ^ k) for i in range(size)])


def block_lists(ncl, nblk, slots, counts):
    cap = nblk // 4

    def body(slots_ref, counts_ref, meta_ref, pos_ref, wanted_ref):
        seq = lax.axis_index("seq")
        cluster = lax.axis_index("cluster")
        meta_ref[0] = seq // 2
        meta_ref[1] = lax.rem(seq, 2)
        meta_ref[2] = cluster
        meta_ref[3] = seq
        valid = [counts_ref[...] > NEAR + j for j in range(REMOTE)]
        ids = [slots_ref[NEAR + j : NEAR + j + 1, :] for j in range(REMOTE)]
        spot = [jnp.zeros((1, nblk), F32) for _ in range(REMOTE)]
        row = lax.broadcasted_iota(jnp.int32, (nblk, nblk), 0)
        before = (row >= lax.broadcasted_iota(jnp.int32, (nblk, nblk), 1)).astype(F32)
        local = lax.broadcasted_iota(jnp.int32, (nblk, 128), 0).astype(F32)
        lane = lax.broadcasted_iota(jnp.int32, (nblk, 128), 1).astype(F32)
        for c in range(ncl):
            hits = [ids[j] - c * nblk == row for j in range(REMOTE)]
            named = jnp.zeros((nblk, nblk), F32)
            for j in range(REMOTE):
                named = jnp.maximum(named, jnp.where(hits[j] & valid[j], 1.0, 0.0))
            present = jnp.max(named, axis=1, keepdims=True)
            wide = jnp.broadcast_to(present, (nblk, 128))
            rank = jnp.dot(before, wide, preferred_element_type=F32) - 1.0
            chosen = jnp.sum(jnp.where((rank == lane) & (wide > 0.0), local, 0.0), axis=0, keepdims=True)
            wanted_ref[c] = jnp.broadcast_to(chosen, (8, 128)).astype(jnp.int32)
            place = rank[:, :nblk] + float(c * cap)
            for j in range(REMOTE):
                spot[j] = spot[j] + jnp.sum(jnp.where(hits[j], place, 0.0), axis=0, keepdims=True)
        for j in range(REMOTE):
            pos_ref[j : j + 1, :] = jnp.where(valid[j], spot[j], spot[0]).astype(jnp.int32)

    return pl.pallas_call(
        body,
        out_shape=[
            jax.ShapeDtypeStruct((4,), jnp.int32),
            jax.ShapeDtypeStruct((REMOTE, nblk), jnp.int32),
            jax.ShapeDtypeStruct((ncl, 8, 128), jnp.int32),
        ],
        in_specs=[VMEM, VMEM],
        out_specs=[SMEM, VMEM, VMEM],
        compiler_params=params(40),
        cost_estimate=cost(0, 4096),
        name="block_lists",
    )(slots, counts.reshape(1, nblk))


def farthest_first(n):
    return sorted(range(1, n), key=lambda k: (-bin(k).count("1"), k))


def exchange(parts, earlier, seq_size):
    parts = list(parts)
    if earlier is not None:
        parts[1], earlier[-1] = lax.optimization_barrier((parts[1], earlier[-1]))
    for j in farthest_first(len(parts)):
        parts[j] = crossed(parts[j], seq_size, 2 * j)
    return parts


def on_device(nodes, w_qkv, w_out, kv_ids, counts):
    seq_size = lax.axis_size("seq")
    ncl = lax.axis_size("cluster")
    heads_dev = HEADS // seq_size
    npair = seq_size // 2
    nblk = seq_size * nodes.shape[0] // BLK
    cap = nblk // 4
    other = crossed(nodes, seq_size, 1)
    slots = kv_ids.T
    meta, pos, wanted = block_lists(ncl, nblk, slots, counts)
    q_span = [(3 * h * HD, HD) for h in range(heads_dev)]
    spans = [[((3 * h + 1) * HD, 2 * HD)] for h in range(heads_dev)]
    (first_kv,) = project(spans[:1], heads_dev, npair, meta, nodes, other, w_qkv)
    wanted, first_kv = lax.optimization_barrier((wanted, first_kv))
    asked = lax.all_to_all(wanted, "cluster", split_axis=0, concat_axis=0, tiled=True)
    (rest,) = project([sum(spans[1:] + [q_span], [])], heads_dev, npair, meta, nodes, other, w_qkv)
    asked, rest = lax.optimization_barrier((asked, rest))
    first_kv = exchange(first_kv, None, seq_size)
    rest = exchange(rest, first_kv, seq_size)
    far = []
    for h in range(heads_dev):
        tables, row = (first_kv, 0) if h == 0 else (rest, (h - 1) * 2 * HD)
        picked = list(select(npair, ncl, cap, meta, asked, tables, row))
        gate = rest[-1] if h == 0 else far[h - 1][0]
        picked[-1], gate = lax.optimization_barrier((picked[-1], gate))
        if h == 0:
            rest[-1] = gate
        else:
            far[h - 1][0] = gate
        far.append([shifted(x, "cluster", ncl, s + 1) for s, x in enumerate(picked)])
    near, stats = near_attention(heads_dev, npair, meta, slots, first_kv, rest)
    outs = far_attention(
        heads_dev, npair, seq_size, ncl, cap, meta, pos, counts, far, rest, near, stats
    )
    pieces = list(outs)
    for k in sorted(range(1, seq_size), key=lambda k: (-bin(k // 2).count("1"), k)):
        pieces[k] = crossed(pieces[k], seq_size, k)
    return project_out(seq_size, meta, pieces, w_out)


def solution(mesh):
    placed = (P(("cluster", "seq"), None), P(), P(), P("cluster", None), P("cluster"))
    return jax.shard_map(
        on_device,
        mesh=mesh,
        in_specs=placed,
        out_specs=P(("cluster", "seq"), None),
        check_vma=False,
    )
```

```python
import jax
import jax.numpy as jnp
from jax import lax
from jax.experimental import pallas as pl
from jax.experimental.pallas import tpu as pltpu
from jax.sharding import PartitionSpec as P

D = 1024
HEADS = 16
HD = 64
BLK = 128
KVB = 16
REMOTE = 4
NEAR = KVB - REMOTE
NEAR_UNROLL = 4
FAR_UNROLL = 8
LOG2E = 1.4426950408889634
F32 = jnp.float32
BF16 = jnp.bfloat16

ANY = pl.BlockSpec(memory_space=pl.ANY)
SMEM = pl.BlockSpec(memory_space=pltpu.SMEM)
VMEM = pl.BlockSpec(memory_space=pltpu.VMEM)


def params(mib):
    return pltpu.CompilerParams(vmem_limit_bytes=mib * 1024 * 1024)


def cost(flops, byts, trans=0):
    return pl.CostEstimate(flops=flops, bytes_accessed=byts, transcendentals=trans)


def nt_dot(a, b):
    return lax.dot_general(a, b, (((1,), (1,)), ((), ())), preferred_element_type=F32)


def place():
    seq = lax.axis_index("seq")
    return seq // 2, lax.rem(seq, 2), lax.axis_index("cluster"), seq


def project(parts, heads_dev, npair, own, other, w_qkv):
    rows = own.shape[0]
    group = 3 * HD * heads_dev
    shared = group % 128 != 0
    slab = 2 * group if shared else group
    top = slab if shared else max(s + n for part in parts for s, n in part)
    width = -(-top // 128) * 128
    heights = [sum(n for _, n in part) for part in parts]
    total = sum(heights)

    def body(own_ref, other_ref, w_ref, *refs):
        outs = refs[: len(parts) * npair]
        x, w, wt, turned, made, sems = refs[len(parts) * npair :]
        pair, core = place()[:2]
        loads = []
        for j in range(npair):
            dest = pair ^ j
            start = dest * slab if shared else (2 * dest + core) * slab
            loads.append(
                pltpu.make_async_copy(
                    w_ref.at[:, pl.ds(pl.multiple_of(start, 128), width)], w.at[j], sems.at[j]
                )
            )
        here = pl.multiple_of(core * rows, 128)
        there = pl.multiple_of((1 - core) * rows, 128)
        loads.append(pltpu.make_async_copy(own_ref, x.at[pl.ds(here, rows)], sems.at[npair]))
        loads.append(pltpu.make_async_copy(other_ref, x.at[pl.ds(there, rows)], sems.at[npair + 1]))
        for load in loads:
            load.start()
        for j in range(npair):
            loads[j].wait()
            if shared:
                turned[...] = w[j].T
            else:
                full = w[j].T
            at = j * total
            for part in parts:
                for s, n in part:
                    if shared:
                        off = pl.multiple_of(core * group + s, HD)
                        wt[at : at + n, :] = turned[pl.ds(off, n), :]
                    else:
                        wt[at : at + n, :] = full[s : s + n, :]
                    at += n
        step = 256
        stores = []
        for half in range(2):
            loads[npair + half].wait()
            for r in range(0, rows, step):
                at_rows = pl.multiple_of((here if half == 0 else there) + r, step)
                res = nt_dot(wt[...], x[pl.ds(at_rows, step), :]).astype(BF16)
                made[:, half * rows + r : half * rows + r + step] = res
                for j in range(npair):
                    at = j * total
                    for k in range(len(parts)):
                        stores.append(
                            pltpu.make_async_copy(
                                made.at[at : at + heights[k], half * rows + r : half * rows + r + step],
                                outs[k * npair + j].at[:, pl.ds(at_rows, step)],
                                sems.at[npair + 2 + len(stores)],
                            )
                        )
                        stores[-1].start()
                        at += heights[k]
        for store in stores:
            store.wait()

    shapes = [jax.ShapeDtypeStruct((heights[k], 2 * rows), BF16) for k in range(len(parts)) for _ in range(npair)]
    outs = pl.pallas_call(
        body,
        out_shape=shapes,
        in_specs=[ANY, ANY, ANY],
        out_specs=[ANY] * len(shapes),
        scratch_shapes=[
            pltpu.VMEM((2 * rows, D), BF16),
            pltpu.VMEM((npair, D, width), BF16),
            pltpu.VMEM((npair * total, D), BF16),
            pltpu.VMEM((width, D) if shared else (16, 128), BF16),
            pltpu.VMEM((npair * total, 2 * rows), BF16),
            pltpu.SemaphoreType.DMA((npair + 2 + npair * len(parts) * 2 * rows // 256,)),
        ],
        compiler_params=params(55),
        cost_estimate=cost(2 * 2 * rows * D * total * npair, 4 * rows * D + 2 * D * width * npair),
        name="project",
    )(own, other, w_qkv)
    return [list(outs[k * npair : (k + 1) * npair]) for k in range(len(parts))]


def select(npair, ncl, cap, asked, tables, row):
    wide = tables[0].shape[1]
    per = wide // BLK

    def body(asked_ref, *refs):
        tabs = refs[:npair]
        outs = refs[npair : npair + ncl - 1]
        held, in_sems, out_sems = refs[npair + ncl - 1 :]
        pair, _, cluster, _ = place()
        loads = [
            pltpu.make_async_copy(tabs[j].at[pl.ds(row, 2 * HD)], held.at[pair ^ j], in_sems.at[j])
            for j in range(npair)
        ]
        for load in loads:
            load.start()
        for load in loads:
            load.wait()
        sends = []
        for s in range(1, ncl):
            for i in range(cap):
                block = asked_ref[lax.rem(cluster + s, ncl), 0, i]
                lane = pl.multiple_of(lax.rem(block, per) * BLK, BLK)
                sends.append(
                    pltpu.make_async_copy(
                        held.at[block // per, :, pl.ds(lane, BLK)],
                        outs[s - 1].at[i],
                        out_sems.at[(s - 1) * cap + i],
                    )
                )
        for send in sends:
            send.start()
        for send in sends:
            send.wait()

    shape = jax.ShapeDtypeStruct((cap, 2 * HD, BLK), BF16)
    return pl.pallas_call(
        body,
        out_shape=[shape] * (ncl - 1),
        in_specs=[SMEM] + [ANY] * npair,
        out_specs=[ANY] * (ncl - 1),
        scratch_shapes=[
            pltpu.VMEM((npair, 2 * HD, wide), BF16),
            pltpu.SemaphoreType.DMA((npair,)),
            pltpu.SemaphoreType.DMA(((ncl - 1) * cap,)),
        ],
        compiler_params=params(40),
        cost_estimate=cost(0, 4 * npair * 2 * HD * wide),
        name="select",
    )(asked, *tables)


def query_matrix(heads_dev, q, per, b):
    lane = pl.multiple_of(lax.rem(b, per) * BLK, BLK)
    x = q[b // per, :, pl.ds(lane, BLK)] * jnp.asarray(HD**-0.5, BF16)
    zero = jnp.zeros((HD, BLK), BF16)
    if heads_dev == 1:
        return jnp.concatenate([x, zero], axis=0)
    left = jnp.concatenate([x[:HD], zero], axis=0)
    right = jnp.concatenate([zero, x[HD:]], axis=0)
    return jnp.concatenate([left, right], axis=1)


def near_attention(heads_dev, npair, ids, first_kv, rest):
    wide = rest[0].shape[1]
    per = wide // BLK
    nblk = npair * per
    feats = heads_dev * HD
    low_q = (heads_dev - 1) * 2 * HD
    cols = heads_dev * BLK
    keys = NEAR * BLK

    def body(ids_ref, *refs):
        tabs = refs[:npair]
        rests = refs[npair : 2 * npair]
        out_ref, stat_ref, kv, q, ktab, vtab, s_a, s_b, t_a, t_b, sems = refs[2 * npair :]
        pair, _, cluster, _ = place()
        base = cluster * nblk
        loads = []
        for j in range(npair):
            at = pair ^ j
            loads.append(pltpu.make_async_copy(tabs[j], kv.at[0, at], sems.at[j]))
            for h in range(1, heads_dev):
                loads.append(
                    pltpu.make_async_copy(
                        rests[j].at[pl.ds((h - 1) * 2 * HD, 2 * HD)], kv.at[h, at], sems.at[h * npair + j]
                    )
                )
            loads.append(
                pltpu.make_async_copy(
                    rests[j].at[pl.ds(low_q, feats)], q.at[at], sems.at[heads_dev * npair + j]
                )
            )
        for load in loads:
            load.start()
        for load in loads:
            load.wait()

        def build(p, carry):
            for i in range(per):
                at = slice(i * BLK, (i + 1) * BLK)
                pieces = [kv[h, p, :, at] for h in range(heads_dev)]
                if heads_dev == 1:
                    ktab[p * per + i] = pieces[0].T
                else:
                    ktab[p * per + i] = jnp.concatenate([x[:HD] for x in pieces], axis=0).T
                vtab[p * per + i] = jnp.concatenate([x[HD:] for x in pieces], axis=0)
            return carry

        lax.fori_loop(0, npair, build, 0)

        def scores(b, qm, held, c, best):
            for j in range(c, c + 4):
                s = jnp.dot(ktab[ids_ref[j, b] - base], qm, preferred_element_type=F32)
                held[j * BLK : (j + 1) * BLK, :] = s
                part = jnp.max(s.reshape(BLK // 8, 8, cols), axis=0)
                best = part if best is None else jnp.maximum(best, part)
            return best

        def values(b, held, top, c, acc, total):
            p = jnp.exp2((held[c * BLK : (c + 4) * BLK, :] - top) * LOG2E)
            part = jnp.sum(p.reshape(4 * BLK // 8, 8, cols), axis=0)
            v = jnp.concatenate([vtab[ids_ref[c + i, b] - base] for i in range(4)], axis=1)
            o = jnp.dot(v, p.astype(BF16), preferred_element_type=F32)
            return (o, part) if acc is None else (acc + o, total + part)

        def stage(start, held, top_ref, held_after, top_after):
            for u in range(NEAR_UNROLL):
                b = start + u
                after = jnp.minimum(b + NEAR_UNROLL, nblk - 1)
                qm = query_matrix(heads_dev, q, per, after)
                top = top_ref[u]
                acc = total = best = None
                for c in range(0, NEAR, 4):
                    best = scores(after, qm, held_after.at[u], c, best)
                    acc, total = values(b, held.at[u], top, c, acc, total)
                top_after[u] = jnp.max(best, axis=0, keepdims=True)
                out_ref[b] = jnp.concatenate(
                    [acc[h * HD : (h + 1) * HD, h * BLK : (h + 1) * BLK] for h in range(heads_dev)],
                    axis=0,
                )
                stat_ref[b, 0:1, :] = top
                stat_ref[b, 1:2, :] = jnp.sum(total, axis=0, keepdims=True)

        for u in range(NEAR_UNROLL):
            qm = query_matrix(heads_dev, q, per, u)
            best = None
            for c in range(0, NEAR, 4):
                best = scores(u, qm, s_a.at[u], c, best)
            t_a[u] = jnp.max(best, axis=0, keepdims=True)

        def step(n, carry):
            b = n * NEAR_UNROLL
            pl.when(lax.rem(n, 2) == 0)(lambda: stage(b, s_a, t_a, s_b, t_b))
            pl.when(lax.rem(n, 2) == 1)(lambda: stage(b, s_b, t_b, s_a, t_a))
            return carry

        lax.fori_loop(0, nblk // NEAR_UNROLL, step, 0)

    flops = nblk * keys * BLK * feats * 4 * heads_dev
    return pl.pallas_call(
        body,
        out_shape=[
            jax.ShapeDtypeStruct((nblk, feats, BLK), F32),
            jax.ShapeDtypeStruct((nblk, 8, cols), F32),
        ],
        in_specs=[SMEM] + [ANY] * (2 * npair),
        out_specs=[VMEM, VMEM],
        scratch_shapes=[
            pltpu.VMEM((heads_dev, npair, 2 * HD, wide), BF16),
            pltpu.VMEM((npair, feats, wide), BF16),
            pltpu.VMEM((nblk, BLK, 2 * HD), BF16),
            pltpu.VMEM((nblk, feats, BLK), BF16),
            pltpu.VMEM((NEAR_UNROLL, keys, cols), F32),
            pltpu.VMEM((NEAR_UNROLL, keys, cols), F32),
            pltpu.VMEM((NEAR_UNROLL, 1, cols), F32),
            pltpu.VMEM((NEAR_UNROLL, 1, cols), F32),
            pltpu.SemaphoreType.DMA((npair * (heads_dev + 1),)),
        ],
        compiler_params=params(40),
        cost_estimate=cost(2 * flops, 8 * nblk * BLK * feats, nblk * keys * cols),
        name="near_attention",
    )(ids, *first_kv, *rest)


def far_attention(heads_dev, npair, seq_size, ncl, cap, pos, counts, tables, rest, near, stats):
    wide = rest[0].shape[1]
    per = wide // BLK
    nblk = npair * per
    low_q = (heads_dev - 1) * 2 * HD
    dev_blocks = nblk // seq_size
    feats = heads_dev * HD
    cols = heads_dev * BLK
    keys = REMOTE * BLK
    shifts = ncl - 1

    def body(pos_ref, counts_ref, *refs):
        tabs = refs[: heads_dev * shifts]
        refs = refs[heads_dev * shifts :]
        rests = refs[:npair]
        near_ref, stat_ref = refs[npair : npair + 2]
        outs = refs[npair + 2 : npair + 2 + seq_size]
        kv, q, ktab, vtab, old, s_a, s_b, t_a, t_b, att, sems = refs[npair + 2 + seq_size :]
        pair, _, cluster, seq = place()
        loads = []
        for h in range(heads_dev):
            for s in range(shifts):
                origin = lax.rem(cluster + ncl - 1 - s, ncl) * cap
                n = h * shifts + s
                loads.append(pltpu.make_async_copy(tabs[n], kv.at[h, pl.ds(origin, cap)], sems.at[n]))
        for j in range(npair):
            loads.append(
                pltpu.make_async_copy(
                    rests[j].at[pl.ds(low_q, feats)], q.at[pair ^ j], sems.at[heads_dev * shifts + j]
                )
            )
        late = []
        for k in range(seq_size):
            at = pl.ds((seq ^ k) * dev_blocks, dev_blocks)
            late.append(
                pltpu.make_async_copy(near_ref.at[at], old.at[at], sems.at[heads_dev * shifts + npair + k])
            )
        for load in loads + late:
            load.start()
        for load in loads:
            load.wait()

        def build(s, carry):
            origin = lax.rem(cluster + ncl - s, ncl) * cap
            for i in range(cap):
                pieces = [kv[h, origin + i] for h in range(heads_dev)]
                if heads_dev == 1:
                    ktab[origin + i] = pieces[0].T
                else:
                    ktab[origin + i] = jnp.concatenate([x[:HD] for x in pieces], axis=0).T
                vtab[origin + i] = jnp.concatenate([x[HD:] for x in pieces], axis=0)
            return carry

        lax.fori_loop(1, ncl, build, 0)

        for load in late:
            load.wait()

        def block_of(n):
            return (seq ^ (n // dev_blocks)) * dev_blocks + lax.rem(n, dev_blocks)

        def scores(b, qm, held, c, best):
            valid = counts_ref[b] - NEAR
            for j in range(c, c + 4):
                s = jnp.dot(ktab[pos_ref[j, b]], qm, preferred_element_type=F32)
                if j:
                    s = jnp.where(j < valid, s, -1e30)
                held[j * BLK : (j + 1) * BLK, :] = s
                part = jnp.max(s.reshape(BLK // 8, 8, cols), axis=0)
                best = part if best is None else jnp.maximum(best, part)
            return best

        def values(b, held, top, c, acc, total):
            p = jnp.exp2((held[c * BLK : (c + 4) * BLK, :] - top) * LOG2E)
            part = jnp.sum(p.reshape(4 * BLK // 8, 8, cols), axis=0)
            v = jnp.concatenate([vtab[pos_ref[c + i, b]] for i in range(4)], axis=1)
            o = jnp.dot(v, p.astype(BF16), preferred_element_type=F32)
            return (o, part) if acc is None else (acc + o, total + part)

        def stage(start, held, top_ref, held_after, top_after):
            for u in range(FAR_UNROLL):
                n = start + u
                b = block_of(n)
                after = block_of(jnp.minimum(n + FAR_UNROLL, nblk - 1))
                qm = query_matrix(heads_dev, q, per, after)
                was = stat_ref[b, 0:1, :]
                top = jnp.maximum(was, top_ref[u])
                acc = total_f = best = None
                for c in range(0, REMOTE, 4):
                    best = scores(after, qm, held_after.at[u], c, best)
                    acc, total_f = values(b, held.at[u], top, c, acc, total_f)
                top_after[u] = jnp.max(best, axis=0, keepdims=True)
                fade = jnp.exp2((was - top) * LOG2E)
                inv = 1.0 / (stat_ref[b, 1:2, :] * fade + jnp.sum(total_f, axis=0, keepdims=True))
                kept = fade * inv
                res = []
                for h in range(heads_dev):
                    at, lane = slice(h * HD, (h + 1) * HD), slice(h * BLK, (h + 1) * BLK)
                    res.append(acc[at, lane] * inv[:, lane] + old[b, at, :] * kept[:, lane])
                att[n] = jnp.concatenate(res, axis=0).astype(BF16)

        for u in range(FAR_UNROLL):
            b = block_of(u)
            qm = query_matrix(heads_dev, q, per, b)
            best = None
            for c in range(0, REMOTE, 4):
                best = scores(b, qm, s_a.at[u], c, best)
            t_a[u] = jnp.max(best, axis=0, keepdims=True)

        def step(i, carry):
            n = i * FAR_UNROLL
            pl.when(lax.rem(i, 2) == 0)(lambda: stage(n, s_a, t_a, s_b, t_b))
            pl.when(lax.rem(i, 2) == 1)(lambda: stage(n, s_b, t_b, s_a, t_a))
            return carry

        lax.fori_loop(0, nblk // FAR_UNROLL, step, 0)
        for k in range(seq_size):
            for i in range(dev_blocks):
                outs[k][:, i * BLK : (i + 1) * BLK] = att[k * dev_blocks + i]

    flops = nblk * keys * BLK * feats * 4 * heads_dev
    return pl.pallas_call(
        body,
        out_shape=[jax.ShapeDtypeStruct((feats, dev_blocks * BLK), BF16)] * seq_size,
        in_specs=[SMEM, SMEM] + [ANY] * (heads_dev * shifts + npair) + [ANY, VMEM],
        out_specs=[VMEM] * seq_size,
        scratch_shapes=[
            pltpu.VMEM((heads_dev, ncl * cap, 2 * HD, BLK), BF16),
            pltpu.VMEM((npair, feats, wide), BF16),
            pltpu.VMEM((ncl * cap, BLK, 2 * HD), BF16),
            pltpu.VMEM((ncl * cap, feats, BLK), BF16),
            pltpu.VMEM((nblk, feats, BLK), F32),
            pltpu.VMEM((FAR_UNROLL, keys, cols), F32),
            pltpu.VMEM((FAR_UNROLL, keys, cols), F32),
            pltpu.VMEM((FAR_UNROLL, 1, cols), F32),
            pltpu.VMEM((FAR_UNROLL, 1, cols), F32),
            pltpu.VMEM((nblk, feats, BLK), BF16),
            pltpu.SemaphoreType.DMA((heads_dev * shifts + npair + seq_size,)),
        ],
        compiler_params=params(40),
        cost_estimate=cost(flops, 6 * nblk * BLK * feats, nblk * keys * cols),
        name="far_attention",
    )(pos, counts, *[x for t in tables for x in t], *rest, near, stats)


def project_out(seq_size, pieces, w_out):
    feats, rows = pieces[0].shape
    step = 128

    def body(*refs):
        parts = refs[:seq_size]
        w_ref, out_ref, at, out, sems = refs[seq_size:]
        seq = place()[3]
        loads = []
        for k in range(seq_size):
            row = pl.multiple_of((seq ^ k) * feats, feats)
            loads.append(pltpu.make_async_copy(parts[k], at.at[pl.ds(row, feats)], sems.at[k]))
        for load in loads:
            load.start()
        for load in loads:
            load.wait()
        stores = []
        for n, r in enumerate(range(0, rows, step)):
            out[r : r + step, :] = jnp.dot(
                at[:, r : r + step].T, w_ref[...], preferred_element_type=F32
            ).astype(BF16)
            rows_at = pl.ds(r, step)
            stores.append(pltpu.make_async_copy(out.at[rows_at], out_ref.at[rows_at], sems.at[seq_size + n]))
            stores[-1].start()
        for store in stores:
            store.wait()

    return pl.pallas_call(
        body,
        out_shape=jax.ShapeDtypeStruct((rows, D), BF16),
        in_specs=[ANY] * seq_size + [VMEM],
        out_specs=ANY,
        scratch_shapes=[
            pltpu.VMEM((HEADS * HD, rows), BF16),
            pltpu.VMEM((rows, D), BF16),
            pltpu.SemaphoreType.DMA((seq_size + rows // step,)),
        ],
        compiler_params=params(40),
        cost_estimate=cost(2 * rows * D * D, 2 * D * D + 4 * rows * D),
        name="project_out",
    )(*pieces, w_out)


def shifted(x, axis, size, shift):
    return lax.ppermute(x, axis, [(i, (i + shift) % size) for i in range(size)])


def crossed(x, size, k):
    return lax.ppermute(x, "seq", [(i, i ^ k) for i in range(size)])


def block_lists(ncl, nblk, slots, counts):
    cap = nblk // 4

    def body(slots_ref, counts_ref, pos_ref, wanted_ref):
        valid = [counts_ref[...] > NEAR + j for j in range(REMOTE)]
        ids = [slots_ref[NEAR + j : NEAR + j + 1, :] for j in range(REMOTE)]
        spot = [jnp.zeros((1, nblk), F32) for _ in range(REMOTE)]
        row = lax.broadcasted_iota(jnp.int32, (nblk, nblk), 0)
        before = (row >= lax.broadcasted_iota(jnp.int32, (nblk, nblk), 1)).astype(F32)
        local = lax.broadcasted_iota(jnp.int32, (nblk, 128), 0).astype(F32)
        lane = lax.broadcasted_iota(jnp.int32, (nblk, 128), 1).astype(F32)
        for c in range(ncl):
            hits = [ids[j] - c * nblk == row for j in range(REMOTE)]
            named = jnp.zeros((nblk, nblk), F32)
            for j in range(REMOTE):
                named = jnp.maximum(named, jnp.where(hits[j] & valid[j], 1.0, 0.0))
            present = jnp.max(named, axis=1, keepdims=True)
            wide = jnp.broadcast_to(present, (nblk, 128))
            rank = jnp.dot(before, wide, preferred_element_type=F32) - 1.0
            chosen = jnp.sum(jnp.where((rank == lane) & (wide > 0.0), local, 0.0), axis=0, keepdims=True)
            wanted_ref[c] = jnp.broadcast_to(chosen, (8, 128)).astype(jnp.int32)
            place = rank[:, :nblk] + float(c * cap)
            for j in range(REMOTE):
                spot[j] = spot[j] + jnp.sum(jnp.where(hits[j], place, 0.0), axis=0, keepdims=True)
        for j in range(REMOTE):
            pos_ref[j : j + 1, :] = jnp.where(valid[j], spot[j], spot[0]).astype(jnp.int32)

    return pl.pallas_call(
        body,
        out_shape=[
            jax.ShapeDtypeStruct((REMOTE, nblk), jnp.int32),
            jax.ShapeDtypeStruct((ncl, 8, 128), jnp.int32),
        ],
        in_specs=[VMEM, VMEM],
        out_specs=[VMEM, VMEM],
        compiler_params=params(40),
        cost_estimate=cost(0, 4096),
        name="block_lists",
    )(slots, counts.reshape(1, nblk))


def farthest_first(n):
    return sorted(range(1, n), key=lambda k: (-bin(k).count("1"), k))


def exchange(parts, earlier, seq_size):
    parts = list(parts)
    if earlier is not None:
        parts[1], earlier[-1] = lax.optimization_barrier((parts[1], earlier[-1]))
    for j in farthest_first(len(parts)):
        parts[j] = crossed(parts[j], seq_size, 2 * j)
    return parts


def on_device(nodes, w_qkv, w_out, kv_ids, counts):
    seq_size = lax.axis_size("seq")
    ncl = lax.axis_size("cluster")
    heads_dev = HEADS // seq_size
    npair = seq_size // 2
    nblk = seq_size * nodes.shape[0] // BLK
    cap = nblk // 4
    other = crossed(nodes, seq_size, 1)
    slots = kv_ids.T
    pos, wanted = block_lists(ncl, nblk, slots, counts)
    q_span = [(3 * h * HD, HD) for h in range(heads_dev)]
    spans = [[((3 * h + 1) * HD, 2 * HD)] for h in range(heads_dev)]
    (first_kv,) = project(spans[:1], heads_dev, npair, nodes, other, w_qkv)
    wanted, first_kv[0] = lax.optimization_barrier((wanted, first_kv[0]))
    asked = lax.all_to_all(wanted, "cluster", split_axis=0, concat_axis=0, tiled=True)
    (rest,) = project([sum(spans[1:] + [q_span], [])], heads_dev, npair, nodes, other, w_qkv)
    asked, rest = lax.optimization_barrier((asked, rest))
    first_kv = exchange(first_kv, None, seq_size)
    rest = exchange(rest, first_kv, seq_size)
    far = []
    for h in range(heads_dev):
        tables, row = (first_kv, 0) if h == 0 else (rest, (h - 1) * 2 * HD)
        picked = list(select(npair, ncl, cap, asked, tables, row))
        gate = rest[-1] if h == 0 else far[h - 1][0]
        picked[-1], gate = lax.optimization_barrier((picked[-1], gate))
        if h == 0:
            rest[-1] = gate
        else:
            far[h - 1][0] = gate
        far.append([shifted(x, "cluster", ncl, s + 1) for s, x in enumerate(picked)])
    near, stats = near_attention(heads_dev, npair, slots, first_kv, rest)
    outs = far_attention(
        heads_dev, npair, seq_size, ncl, cap, pos, counts, far, rest, near, stats
    )
    pieces = list(outs)
    for k in sorted(range(1, seq_size), key=lambda k: (-bin(k // 2).count("1"), k)):
        pieces[k] = crossed(pieces[k], seq_size, k)
    return project_out(seq_size, pieces, w_out)


def solution(mesh):
    placed = (P(("cluster", "seq"), None), P(), P(), P("cluster", None), P("cluster"))
    return jax.shard_map(
        on_device,
        mesh=mesh,
        in_specs=placed,
        out_specs=P(("cluster", "seq"), None),
        check_vma=False,
    )
```

```python
import jax
import jax.numpy as jnp
from jax import lax
from jax.experimental import pallas as pl
from jax.experimental.pallas import tpu as pltpu
from jax.sharding import PartitionSpec as P

D = 1024
HEADS = 16
HD = 64
BLK = 128
KVB = 16
REMOTE = 4
NEAR = KVB - REMOTE
NEAR_UNROLL = 4
FAR_UNROLL = 8
LOG2E = 1.4426950408889634
F32 = jnp.float32
BF16 = jnp.bfloat16

ANY = pl.BlockSpec(memory_space=pl.ANY)
SMEM = pl.BlockSpec(memory_space=pltpu.SMEM)
VMEM = pl.BlockSpec(memory_space=pltpu.VMEM)


def params(mib):
    return pltpu.CompilerParams(vmem_limit_bytes=mib * 1024 * 1024)


def cost(flops, byts, trans=0):
    return pl.CostEstimate(flops=flops, bytes_accessed=byts, transcendentals=trans)


def nt_dot(a, b):
    return lax.dot_general(a, b, (((1,), (1,)), ((), ())), preferred_element_type=F32)


def place():
    seq = lax.axis_index("seq")
    return seq // 2, lax.rem(seq, 2), lax.axis_index("cluster"), seq


def project(parts, heads_dev, npair, own, other, w_qkv):
    rows = own.shape[0]
    group = 3 * HD * heads_dev
    shared = group % 128 != 0
    slab = 2 * group if shared else group
    top = slab if shared else max(s + n for part in parts for s, n in part)
    width = -(-top // 128) * 128
    heights = [sum(n for _, n in part) for part in parts]
    total = sum(heights)

    def body(own_ref, other_ref, w_ref, *refs):
        outs = refs[: len(parts) * npair]
        x, w, wt, turned, made, sems = refs[len(parts) * npair :]
        pair, core = place()[:2]
        loads = []
        for j in range(npair):
            dest = pair ^ j
            start = dest * slab if shared else (2 * dest + core) * slab
            loads.append(
                pltpu.make_async_copy(
                    w_ref.at[:, pl.ds(pl.multiple_of(start, 128), width)], w.at[j], sems.at[j]
                )
            )
        here = pl.multiple_of(core * rows, 128)
        there = pl.multiple_of((1 - core) * rows, 128)
        loads.append(pltpu.make_async_copy(own_ref, x.at[pl.ds(here, rows)], sems.at[npair]))
        loads.append(pltpu.make_async_copy(other_ref, x.at[pl.ds(there, rows)], sems.at[npair + 1]))
        for load in loads:
            load.start()
        for j in range(npair):
            loads[j].wait()
            if shared:
                turned[...] = w[j].T
            else:
                full = w[j].T
            at = j * total
            for part in parts:
                for s, n in part:
                    if shared:
                        off = pl.multiple_of(core * group + s, HD)
                        wt[at : at + n, :] = turned[pl.ds(off, n), :]
                    else:
                        wt[at : at + n, :] = full[s : s + n, :]
                    at += n
        step = 256
        stores = []
        for half in range(2):
            loads[npair + half].wait()
            for r in range(0, rows, step):
                at_rows = pl.multiple_of((here if half == 0 else there) + r, step)
                res = nt_dot(wt[...], x[pl.ds(at_rows, step), :]).astype(BF16)
                made[:, half * rows + r : half * rows + r + step] = res
                for j in range(npair):
                    at = j * total
                    for k in range(len(parts)):
                        stores.append(
                            pltpu.make_async_copy(
                                made.at[at : at + heights[k], half * rows + r : half * rows + r + step],
                                outs[k * npair + j].at[:, pl.ds(at_rows, step)],
                                sems.at[npair + 2 + len(stores)],
                            )
                        )
                        stores[-1].start()
                        at += heights[k]
        for store in stores:
            store.wait()

    shapes = [jax.ShapeDtypeStruct((heights[k], 2 * rows), BF16) for k in range(len(parts)) for _ in range(npair)]
    outs = pl.pallas_call(
        body,
        out_shape=shapes,
        in_specs=[ANY, ANY, ANY],
        out_specs=[ANY] * len(shapes),
        scratch_shapes=[
            pltpu.VMEM((2 * rows, D), BF16),
            pltpu.VMEM((npair, D, width), BF16),
            pltpu.VMEM((npair * total, D), BF16),
            pltpu.VMEM((width, D) if shared else (16, 128), BF16),
            pltpu.VMEM((npair * total, 2 * rows), BF16),
            pltpu.SemaphoreType.DMA((npair + 2 + npair * len(parts) * 2 * rows // 256,)),
        ],
        compiler_params=params(55),
        cost_estimate=cost(2 * 2 * rows * D * total * npair, 4 * rows * D + 2 * D * width * npair),
        name="project",
    )(own, other, w_qkv)
    return [list(outs[k * npair : (k + 1) * npair]) for k in range(len(parts))]


def select(npair, ncl, cap, asked, tables, row):
    wide = tables[0].shape[1]
    per = wide // BLK

    def body(asked_ref, *refs):
        tabs = refs[:npair]
        outs = refs[npair : npair + ncl - 1]
        held, in_sems, out_sems = refs[npair + ncl - 1 :]
        pair, _, cluster, _ = place()
        loads = [
            pltpu.make_async_copy(tabs[j].at[pl.ds(row, 2 * HD)], held.at[pair ^ j], in_sems.at[j])
            for j in range(npair)
        ]
        for load in loads:
            load.start()
        for load in loads:
            load.wait()
        sends = []
        for s in range(1, ncl):
            for i in range(cap):
                block = asked_ref[lax.rem(cluster + s, ncl), 0, i]
                lane = pl.multiple_of(lax.rem(block, per) * BLK, BLK)
                sends.append(
                    pltpu.make_async_copy(
                        held.at[block // per, :, pl.ds(lane, BLK)],
                        outs[s - 1].at[i],
                        out_sems.at[(s - 1) * cap + i],
                    )
                )
        for send in sends:
            send.start()
        for send in sends:
            send.wait()

    shape = jax.ShapeDtypeStruct((cap, 2 * HD, BLK), BF16)
    return pl.pallas_call(
        body,
        out_shape=[shape] * (ncl - 1),
        in_specs=[SMEM] + [ANY] * npair,
        out_specs=[ANY] * (ncl - 1),
        scratch_shapes=[
            pltpu.VMEM((npair, 2 * HD, wide), BF16),
            pltpu.SemaphoreType.DMA((npair,)),
            pltpu.SemaphoreType.DMA(((ncl - 1) * cap,)),
        ],
        compiler_params=params(40),
        cost_estimate=cost(0, 4 * npair * 2 * HD * wide),
        name="select",
    )(asked, *tables)


def query_matrix(heads_dev, q, per, b):
    lane = pl.multiple_of(lax.rem(b, per) * BLK, BLK)
    x = q[b // per, :, pl.ds(lane, BLK)] * jnp.asarray(HD**-0.5, BF16)
    zero = jnp.zeros((HD, BLK), BF16)
    if heads_dev == 1:
        return jnp.concatenate([x, zero], axis=0)
    left = jnp.concatenate([x[:HD], zero], axis=0)
    right = jnp.concatenate([zero, x[HD:]], axis=0)
    return jnp.concatenate([left, right], axis=1)


def near_attention(heads_dev, npair, ids, first_kv, rest):
    wide = rest[0].shape[1]
    per = wide // BLK
    nblk = npair * per
    feats = heads_dev * HD
    low_q = (heads_dev - 1) * 2 * HD
    cols = heads_dev * BLK
    keys = NEAR * BLK

    def body(ids_ref, *refs):
        tabs = refs[:npair]
        rests = refs[npair : 2 * npair]
        out_ref, stat_ref, kv, q, ktab, vtab, s_a, s_b, t_a, t_b, sems = refs[2 * npair :]
        pair, _, cluster, _ = place()
        base = cluster * nblk
        loads = []
        for j in range(npair):
            at = pair ^ j
            loads.append(pltpu.make_async_copy(tabs[j], kv.at[0, at], sems.at[j]))
            for h in range(1, heads_dev):
                loads.append(
                    pltpu.make_async_copy(
                        rests[j].at[pl.ds((h - 1) * 2 * HD, 2 * HD)], kv.at[h, at], sems.at[h * npair + j]
                    )
                )
            loads.append(
                pltpu.make_async_copy(
                    rests[j].at[pl.ds(low_q, feats)], q.at[at], sems.at[heads_dev * npair + j]
                )
            )
        for load in loads:
            load.start()
        for load in loads:
            load.wait()

        def build(p, carry):
            for i in range(per):
                at = slice(i * BLK, (i + 1) * BLK)
                pieces = [kv[h, p, :, at] for h in range(heads_dev)]
                if heads_dev == 1:
                    ktab[p * per + i] = pieces[0].T
                else:
                    ktab[p * per + i] = jnp.concatenate([x[:HD] for x in pieces], axis=0).T
                vtab[p * per + i] = jnp.concatenate([x[HD:] for x in pieces], axis=0)
            return carry

        lax.fori_loop(0, npair, build, 0)

        def scores(b, qm, held, c, best):
            for j in range(c, c + 4):
                s = jnp.dot(ktab[ids_ref[j, b] - base], qm, preferred_element_type=F32)
                held[j * BLK : (j + 1) * BLK, :] = s
                part = jnp.max(s.reshape(BLK // 8, 8, cols), axis=0)
                best = part if best is None else jnp.maximum(best, part)
            return best

        def values(b, held, top, c, acc, total):
            p = jnp.exp2((held[c * BLK : (c + 4) * BLK, :] - top) * LOG2E)
            part = jnp.sum(p.reshape(4 * BLK // 8, 8, cols), axis=0)
            v = jnp.concatenate([vtab[ids_ref[c + i, b] - base] for i in range(4)], axis=1)
            o = jnp.dot(v, p.astype(BF16), preferred_element_type=F32)
            return (o, part) if acc is None else (acc + o, total + part)

        def stage(start, held, top_ref, held_after, top_after):
            for u in range(NEAR_UNROLL):
                b = start + u
                after = jnp.minimum(b + NEAR_UNROLL, nblk - 1)
                qm = query_matrix(heads_dev, q, per, after)
                top = top_ref[u]
                acc = total = best = None
                for c in range(0, NEAR, 4):
                    best = scores(after, qm, held_after.at[u], c, best)
                    acc, total = values(b, held.at[u], top, c, acc, total)
                top_after[u] = jnp.max(best, axis=0, keepdims=True)
                out_ref[b] = jnp.concatenate(
                    [acc[h * HD : (h + 1) * HD, h * BLK : (h + 1) * BLK] for h in range(heads_dev)],
                    axis=0,
                )
                stat_ref[b, 0:1, :] = top
                stat_ref[b, 1:2, :] = jnp.sum(total, axis=0, keepdims=True)

        for u in range(NEAR_UNROLL):
            qm = query_matrix(heads_dev, q, per, u)
            best = None
            for c in range(0, NEAR, 4):
                best = scores(u, qm, s_a.at[u], c, best)
            t_a[u] = jnp.max(best, axis=0, keepdims=True)

        def step(n, carry):
            b = n * NEAR_UNROLL
            pl.when(lax.rem(n, 2) == 0)(lambda: stage(b, s_a, t_a, s_b, t_b))
            pl.when(lax.rem(n, 2) == 1)(lambda: stage(b, s_b, t_b, s_a, t_a))
            return carry

        lax.fori_loop(0, nblk // NEAR_UNROLL, step, 0)

    flops = nblk * keys * BLK * feats * 4 * heads_dev
    return pl.pallas_call(
        body,
        out_shape=[
            jax.ShapeDtypeStruct((nblk, feats, BLK), F32),
            jax.ShapeDtypeStruct((nblk, 8, cols), F32),
        ],
        in_specs=[SMEM] + [ANY] * (2 * npair),
        out_specs=[VMEM, VMEM],
        scratch_shapes=[
            pltpu.VMEM((heads_dev, npair, 2 * HD, wide), BF16),
            pltpu.VMEM((npair, feats, wide), BF16),
            pltpu.VMEM((nblk, BLK, 2 * HD), BF16),
            pltpu.VMEM((nblk, feats, BLK), BF16),
            pltpu.VMEM((NEAR_UNROLL, keys, cols), F32),
            pltpu.VMEM((NEAR_UNROLL, keys, cols), F32),
            pltpu.VMEM((NEAR_UNROLL, 1, cols), F32),
            pltpu.VMEM((NEAR_UNROLL, 1, cols), F32),
            pltpu.SemaphoreType.DMA((npair * (heads_dev + 1),)),
        ],
        compiler_params=params(40),
        cost_estimate=cost(2 * flops, 8 * nblk * BLK * feats, nblk * keys * cols),
        name="near_attention",
    )(ids, *first_kv, *rest)


def far_attention(heads_dev, npair, seq_size, ncl, cap, pos, counts, tables, rest, near, stats):
    wide = rest[0].shape[1]
    per = wide // BLK
    nblk = npair * per
    low_q = (heads_dev - 1) * 2 * HD
    dev_blocks = nblk // seq_size
    feats = heads_dev * HD
    cols = heads_dev * BLK
    keys = REMOTE * BLK
    shifts = ncl - 1

    def body(pos_ref, counts_ref, *refs):
        tabs = refs[: heads_dev * shifts]
        refs = refs[heads_dev * shifts :]
        rests = refs[:npair]
        near_ref, stat_ref = refs[npair : npair + 2]
        outs = refs[npair + 2 : npair + 2 + seq_size]
        kv, q, ktab, vtab, old, s_a, s_b, t_a, t_b, att, sems = refs[npair + 2 + seq_size :]
        pair, _, cluster, seq = place()
        loads = []
        for h in range(heads_dev):
            for s in range(shifts):
                origin = lax.rem(cluster + ncl - 1 - s, ncl) * cap
                n = h * shifts + s
                loads.append(pltpu.make_async_copy(tabs[n], kv.at[h, pl.ds(origin, cap)], sems.at[n]))
        for j in range(npair):
            loads.append(
                pltpu.make_async_copy(
                    rests[j].at[pl.ds(low_q, feats)], q.at[pair ^ j], sems.at[heads_dev * shifts + j]
                )
            )
        late = []
        for k in range(seq_size):
            at = pl.ds((seq ^ k) * dev_blocks, dev_blocks)
            late.append(
                pltpu.make_async_copy(near_ref.at[at], old.at[at], sems.at[heads_dev * shifts + npair + k])
            )
        for load in loads + late:
            load.start()
        for load in loads:
            load.wait()

        def build(s, carry):
            origin = lax.rem(cluster + ncl - s, ncl) * cap
            for i in range(cap):
                pieces = [kv[h, origin + i] for h in range(heads_dev)]
                if heads_dev == 1:
                    ktab[origin + i] = pieces[0].T
                else:
                    ktab[origin + i] = jnp.concatenate([x[:HD] for x in pieces], axis=0).T
                vtab[origin + i] = jnp.concatenate([x[HD:] for x in pieces], axis=0)
            return carry

        lax.fori_loop(1, ncl, build, 0)

        for load in late:
            load.wait()

        def block_of(n):
            return (seq ^ (n // dev_blocks)) * dev_blocks + lax.rem(n, dev_blocks)

        def scores(b, qm, held, c, best):
            valid = counts_ref[b] - NEAR
            for j in range(c, c + 4):
                s = jnp.dot(ktab[pos_ref[j, b]], qm, preferred_element_type=F32)
                if j:
                    s = jnp.where(j < valid, s, -1e30)
                held[j * BLK : (j + 1) * BLK, :] = s
                part = jnp.max(s.reshape(BLK // 8, 8, cols), axis=0)
                best = part if best is None else jnp.maximum(best, part)
            return best

        def values(b, held, top, c, acc, total):
            p = jnp.exp2((held[c * BLK : (c + 4) * BLK, :] - top) * LOG2E)
            part = jnp.sum(p.reshape(4 * BLK // 8, 8, cols), axis=0)
            v = jnp.concatenate([vtab[pos_ref[c + i, b]] for i in range(4)], axis=1)
            o = jnp.dot(v, p.astype(BF16), preferred_element_type=F32)
            return (o, part) if acc is None else (acc + o, total + part)

        def stage(start, held, top_ref, held_after, top_after):
            for u in range(FAR_UNROLL):
                n = start + u
                b = block_of(n)
                after = block_of(jnp.minimum(n + FAR_UNROLL, nblk - 1))
                qm = query_matrix(heads_dev, q, per, after)
                was = stat_ref[b, 0:1, :]
                top = jnp.maximum(was, top_ref[u])
                acc = total_f = best = None
                for c in range(0, REMOTE, 4):
                    best = scores(after, qm, held_after.at[u], c, best)
                    acc, total_f = values(b, held.at[u], top, c, acc, total_f)
                top_after[u] = jnp.max(best, axis=0, keepdims=True)
                fade = jnp.exp2((was - top) * LOG2E)
                inv = 1.0 / (stat_ref[b, 1:2, :] * fade + jnp.sum(total_f, axis=0, keepdims=True))
                kept = fade * inv
                res = []
                for h in range(heads_dev):
                    at, lane = slice(h * HD, (h + 1) * HD), slice(h * BLK, (h + 1) * BLK)
                    res.append(acc[at, lane] * inv[:, lane] + old[b, at, :] * kept[:, lane])
                att[n] = jnp.concatenate(res, axis=0).astype(BF16)

        for u in range(FAR_UNROLL):
            b = block_of(u)
            qm = query_matrix(heads_dev, q, per, b)
            best = None
            for c in range(0, REMOTE, 4):
                best = scores(b, qm, s_a.at[u], c, best)
            t_a[u] = jnp.max(best, axis=0, keepdims=True)

        def step(i, carry):
            n = i * FAR_UNROLL
            pl.when(lax.rem(i, 2) == 0)(lambda: stage(n, s_a, t_a, s_b, t_b))
            pl.when(lax.rem(i, 2) == 1)(lambda: stage(n, s_b, t_b, s_a, t_a))
            return carry

        lax.fori_loop(0, nblk // FAR_UNROLL, step, 0)
        for k in range(seq_size):
            for i in range(dev_blocks):
                outs[k][:, i * BLK : (i + 1) * BLK] = att[k * dev_blocks + i]

    flops = nblk * keys * BLK * feats * 4 * heads_dev
    return pl.pallas_call(
        body,
        out_shape=[jax.ShapeDtypeStruct((feats, dev_blocks * BLK), BF16)] * seq_size,
        in_specs=[SMEM, SMEM] + [ANY] * (heads_dev * shifts + npair) + [ANY, VMEM],
        out_specs=[VMEM] * seq_size,
        scratch_shapes=[
            pltpu.VMEM((heads_dev, ncl * cap, 2 * HD, BLK), BF16),
            pltpu.VMEM((npair, feats, wide), BF16),
            pltpu.VMEM((ncl * cap, BLK, 2 * HD), BF16),
            pltpu.VMEM((ncl * cap, feats, BLK), BF16),
            pltpu.VMEM((nblk, feats, BLK), F32),
            pltpu.VMEM((FAR_UNROLL, keys, cols), F32),
            pltpu.VMEM((FAR_UNROLL, keys, cols), F32),
            pltpu.VMEM((FAR_UNROLL, 1, cols), F32),
            pltpu.VMEM((FAR_UNROLL, 1, cols), F32),
            pltpu.VMEM((nblk, feats, BLK), BF16),
            pltpu.SemaphoreType.DMA((heads_dev * shifts + npair + seq_size,)),
        ],
        compiler_params=params(40),
        cost_estimate=cost(flops, 6 * nblk * BLK * feats, nblk * keys * cols),
        name="far_attention",
    )(pos, counts, *[x for t in tables for x in t], *rest, near, stats)


def project_out(seq_size, pieces, w_out):
    feats, rows = pieces[0].shape
    step = 128

    def body(*refs):
        parts = refs[:seq_size]
        w_ref, out_ref, at, out, sems = refs[seq_size:]
        seq = place()[3]
        loads = []
        for k in range(seq_size):
            row = pl.multiple_of((seq ^ k) * feats, feats)
            loads.append(pltpu.make_async_copy(parts[k], at.at[pl.ds(row, feats)], sems.at[k]))
        for load in loads:
            load.start()
        for load in loads:
            load.wait()
        stores = []
        for n, r in enumerate(range(0, rows, step)):
            out[r : r + step, :] = jnp.dot(
                at[:, r : r + step].T, w_ref[...], preferred_element_type=F32
            ).astype(BF16)
            rows_at = pl.ds(r, step)
            stores.append(pltpu.make_async_copy(out.at[rows_at], out_ref.at[rows_at], sems.at[seq_size + n]))
            stores[-1].start()
        for store in stores:
            store.wait()

    return pl.pallas_call(
        body,
        out_shape=jax.ShapeDtypeStruct((rows, D), BF16),
        in_specs=[ANY] * seq_size + [VMEM],
        out_specs=ANY,
        scratch_shapes=[
            pltpu.VMEM((HEADS * HD, rows), BF16),
            pltpu.VMEM((rows, D), BF16),
            pltpu.SemaphoreType.DMA((seq_size + rows // step,)),
        ],
        compiler_params=params(40),
        cost_estimate=cost(2 * rows * D * D, 2 * D * D + 4 * rows * D),
        name="project_out",
    )(*pieces, w_out)


def shifted(x, axis, size, shift):
    return lax.ppermute(x, axis, [(i, (i + shift) % size) for i in range(size)])


def crossed(x, size, k):
    return lax.ppermute(x, "seq", [(i, i ^ k) for i in range(size)])


def block_lists(ncl, nblk, slots, counts):
    cap = nblk // 4

    def body(slots_ref, counts_ref, pos_ref, wanted_ref):
        valid = [counts_ref[...] > NEAR + j for j in range(REMOTE)]
        ids = [slots_ref[NEAR + j : NEAR + j + 1, :] for j in range(REMOTE)]
        spot = [jnp.zeros((1, nblk), F32) for _ in range(REMOTE)]
        row = lax.broadcasted_iota(jnp.int32, (nblk, nblk), 0)
        before = (row >= lax.broadcasted_iota(jnp.int32, (nblk, nblk), 1)).astype(F32)
        local = lax.broadcasted_iota(jnp.int32, (nblk, 128), 0).astype(F32)
        lane = lax.broadcasted_iota(jnp.int32, (nblk, 128), 1).astype(F32)
        for c in range(ncl):
            hits = [ids[j] - c * nblk == row for j in range(REMOTE)]
            named = jnp.zeros((nblk, nblk), F32)
            for j in range(REMOTE):
                named = jnp.maximum(named, jnp.where(hits[j] & valid[j], 1.0, 0.0))
            present = jnp.max(named, axis=1, keepdims=True)
            wide = jnp.broadcast_to(present, (nblk, 128))
            rank = jnp.dot(before, wide, preferred_element_type=F32) - 1.0
            chosen = jnp.sum(jnp.where((rank == lane) & (wide > 0.0), local, 0.0), axis=0, keepdims=True)
            wanted_ref[c] = jnp.broadcast_to(chosen, (8, 128)).astype(jnp.int32)
            place = rank[:, :nblk] + float(c * cap)
            for j in range(REMOTE):
                spot[j] = spot[j] + jnp.sum(jnp.where(hits[j], place, 0.0), axis=0, keepdims=True)
        for j in range(REMOTE):
            pos_ref[j : j + 1, :] = jnp.where(valid[j], spot[j], spot[0]).astype(jnp.int32)

    return pl.pallas_call(
        body,
        out_shape=[
            jax.ShapeDtypeStruct((REMOTE, nblk), jnp.int32),
            jax.ShapeDtypeStruct((ncl, 8, 128), jnp.int32),
        ],
        in_specs=[VMEM, VMEM],
        out_specs=[VMEM, VMEM],
        compiler_params=params(40),
        cost_estimate=cost(0, 4096),
        name="block_lists",
    )(slots, counts.reshape(1, nblk))


def farthest_first(n):
    return sorted(range(1, n), key=lambda k: (-bin(k).count("1"), k))


def exchange(parts, earlier, seq_size):
    parts = list(parts)
    if earlier is not None:
        parts[1], earlier[-1] = lax.optimization_barrier((parts[1], earlier[-1]))
    for j in farthest_first(len(parts)):
        parts[j] = crossed(parts[j], seq_size, 2 * j)
    return parts


def on_device(nodes, w_qkv, w_out, kv_ids, counts):
    seq_size = lax.axis_size("seq")
    ncl = lax.axis_size("cluster")
    heads_dev = HEADS // seq_size
    npair = seq_size // 2
    nblk = seq_size * nodes.shape[0] // BLK
    cap = nblk // 4
    other = crossed(nodes, seq_size, 1)
    slots = kv_ids.T
    pos, wanted = block_lists(ncl, nblk, slots, counts)
    q_span = [(3 * h * HD, HD) for h in range(heads_dev)]
    spans = [[((3 * h + 1) * HD, 2 * HD)] for h in range(heads_dev)]
    (first_kv,) = project(spans[:1], heads_dev, npair, nodes, other, w_qkv)
    wanted, first_kv[0] = lax.optimization_barrier((wanted, first_kv[0]))
    asked = lax.all_to_all(wanted, "cluster", split_axis=0, concat_axis=0, tiled=True)
    (rest,) = project([sum(spans[1:] + [q_span], [])], heads_dev, npair, nodes, other, w_qkv)
    asked, rest = lax.optimization_barrier((asked, rest))
    first_kv = exchange(first_kv, None, seq_size)
    rest = exchange(rest, first_kv, seq_size)
    far = []
    for h in range(heads_dev):
        tables, row = (first_kv, 0) if h == 0 else (rest, (h - 1) * 2 * HD)
        picked = list(select(npair, ncl, cap, asked, tables, row))
        order = sorted(range(ncl - 1), key=lambda s: (abs(2 * s + 2 - ncl), -s))
        last = order[-1]
        if h:
            picked[last], far[h - 1][order[1]] = lax.optimization_barrier((picked[last], far[h - 1][order[1]]))
        else:
            picked[last], rest[-1] = lax.optimization_barrier((picked[last], rest[-1]))
        for s in order:
            picked[s] = shifted(picked[s], "cluster", ncl, s + 1)
        far.append(picked)
    near, stats = near_attention(heads_dev, npair, slots, first_kv, rest)
    outs = far_attention(
        heads_dev, npair, seq_size, ncl, cap, pos, counts, far, rest, near, stats
    )
    pieces = list(outs)
    for k in sorted(range(1, seq_size), key=lambda k: (-bin(k // 2).count("1"), k)):
        pieces[k] = crossed(pieces[k], seq_size, k)
    return project_out(seq_size, pieces, w_out)


def solution(mesh):
    placed = (P(("cluster", "seq"), None), P(), P(), P("cluster", None), P("cluster"))
    return jax.shard_map(
        on_device,
        mesh=mesh,
        in_specs=placed,
        out_specs=P(("cluster", "seq"), None),
        check_vma=False,
    )
```

```python
import jax
import jax.numpy as jnp
from jax import lax
from jax.experimental import pallas as pl
from jax.experimental.pallas import tpu as pltpu
from jax.sharding import PartitionSpec as P

D = 1024
HEADS = 16
HD = 64
BLK = 128
KVB = 16
REMOTE = 4
NEAR = KVB - REMOTE
NEAR_UNROLL = 4
FAR_UNROLL = 8
LOG2E = 1.4426950408889634
F32 = jnp.float32
BF16 = jnp.bfloat16

ANY = pl.BlockSpec(memory_space=pl.ANY)
SMEM = pl.BlockSpec(memory_space=pltpu.SMEM)
VMEM = pl.BlockSpec(memory_space=pltpu.VMEM)


def params(mib):
    return pltpu.CompilerParams(vmem_limit_bytes=mib * 1024 * 1024)


def cost(flops, byts, trans=0):
    return pl.CostEstimate(flops=flops, bytes_accessed=byts, transcendentals=trans)


def nt_dot(a, b):
    return lax.dot_general(a, b, (((1,), (1,)), ((), ())), preferred_element_type=F32)


def place():
    seq = lax.axis_index("seq")
    return seq // 2, lax.rem(seq, 2), lax.axis_index("cluster"), seq


def project(parts, heads_dev, npair, own, other, w_qkv):
    rows = own.shape[0]
    group = 3 * HD * heads_dev
    shared = group % 128 != 0
    slab = 2 * group if shared else group
    top = slab if shared else max(s + n for part in parts for s, n in part)
    width = -(-top // 128) * 128
    heights = [sum(n for _, n in part) for part in parts]
    total = sum(heights)

    def body(own_ref, other_ref, w_ref, *refs):
        outs = refs[: len(parts) * npair]
        x, w, wt, turned, made, sems = refs[len(parts) * npair :]
        pair, core = place()[:2]
        loads = []
        for j in range(npair):
            dest = pair ^ j
            start = dest * slab if shared else (2 * dest + core) * slab
            loads.append(
                pltpu.make_async_copy(
                    w_ref.at[:, pl.ds(pl.multiple_of(start, 128), width)], w.at[j], sems.at[j]
                )
            )
        here = pl.multiple_of(core * rows, 128)
        there = pl.multiple_of((1 - core) * rows, 128)
        loads.append(pltpu.make_async_copy(own_ref, x.at[pl.ds(here, rows)], sems.at[npair]))
        loads.append(pltpu.make_async_copy(other_ref, x.at[pl.ds(there, rows)], sems.at[npair + 1]))
        for load in loads:
            load.start()
        for j in range(npair):
            loads[j].wait()
            if shared:
                turned[...] = w[j].T
            else:
                full = w[j].T
            at = j * total
            for part in parts:
                for s, n in part:
                    if shared:
                        off = pl.multiple_of(core * group + s, HD)
                        wt[at : at + n, :] = turned[pl.ds(off, n), :]
                    else:
                        wt[at : at + n, :] = full[s : s + n, :]
                    at += n
        step = 256
        stores = []
        for half in range(2):
            loads[npair + half].wait()
            for r in range(0, rows, step):
                at_rows = pl.multiple_of((here if half == 0 else there) + r, step)
                res = nt_dot(wt[...], x[pl.ds(at_rows, step), :]).astype(BF16)
                made[:, half * rows + r : half * rows + r + step] = res
                for j in range(npair):
                    at = j * total
                    for k in range(len(parts)):
                        stores.append(
                            pltpu.make_async_copy(
                                made.at[at : at + heights[k], half * rows + r : half * rows + r + step],
                                outs[k * npair + j].at[:, pl.ds(at_rows, step)],
                                sems.at[npair + 2 + len(stores)],
                            )
                        )
                        stores[-1].start()
                        at += heights[k]
        for store in stores:
            store.wait()

    shapes = [jax.ShapeDtypeStruct((heights[k], 2 * rows), BF16) for k in range(len(parts)) for _ in range(npair)]
    outs = pl.pallas_call(
        body,
        out_shape=shapes,
        in_specs=[ANY, ANY, ANY],
        out_specs=[ANY] * len(shapes),
        scratch_shapes=[
            pltpu.VMEM((2 * rows, D), BF16),
            pltpu.VMEM((npair, D, width), BF16),
            pltpu.VMEM((npair * total, D), BF16),
            pltpu.VMEM((width, D) if shared else (16, 128), BF16),
            pltpu.VMEM((npair * total, 2 * rows), BF16),
            pltpu.SemaphoreType.DMA((npair + 2 + npair * len(parts) * 2 * rows // 256,)),
        ],
        compiler_params=params(55),
        cost_estimate=cost(2 * 2 * rows * D * total * npair, 4 * rows * D + 2 * D * width * npair),
        name="project",
    )(own, other, w_qkv)
    return [list(outs[k * npair : (k + 1) * npair]) for k in range(len(parts))]


def select(npair, ncl, cap, asked, tables, row):
    wide = tables[0].shape[1]
    per = wide // BLK

    def body(asked_ref, *refs):
        tabs = refs[:npair]
        outs = refs[npair : npair + ncl - 1]
        held, in_sems, out_sems = refs[npair + ncl - 1 :]
        pair, _, cluster, _ = place()
        loads = [
            pltpu.make_async_copy(tabs[j].at[pl.ds(row, 2 * HD)], held.at[pair ^ j], in_sems.at[j])
            for j in range(npair)
        ]
        for load in loads:
            load.start()
        for load in loads:
            load.wait()
        sends = []
        for s in range(1, ncl):
            for i in range(cap):
                block = asked_ref[lax.rem(cluster + s, ncl), 0, i]
                lane = pl.multiple_of(lax.rem(block, per) * BLK, BLK)
                sends.append(
                    pltpu.make_async_copy(
                        held.at[block // per, :, pl.ds(lane, BLK)],
                        outs[s - 1].at[i],
                        out_sems.at[(s - 1) * cap + i],
                    )
                )
        for send in sends:
            send.start()
        for send in sends:
            send.wait()

    shape = jax.ShapeDtypeStruct((cap, 2 * HD, BLK), BF16)
    return pl.pallas_call(
        body,
        out_shape=[shape] * (ncl - 1),
        in_specs=[SMEM] + [ANY] * npair,
        out_specs=[ANY] * (ncl - 1),
        scratch_shapes=[
            pltpu.VMEM((npair, 2 * HD, wide), BF16),
            pltpu.SemaphoreType.DMA((npair,)),
            pltpu.SemaphoreType.DMA(((ncl - 1) * cap,)),
        ],
        compiler_params=params(40),
        cost_estimate=cost(0, 4 * npair * 2 * HD * wide),
        name="select",
    )(asked, *tables)


def query_matrix(heads_dev, q, per, b):
    lane = pl.multiple_of(lax.rem(b, per) * BLK, BLK)
    x = q[b // per, :, pl.ds(lane, BLK)] * jnp.asarray(HD**-0.5, BF16)
    zero = jnp.zeros((HD, BLK), BF16)
    if heads_dev == 1:
        return jnp.concatenate([x, zero], axis=0)
    left = jnp.concatenate([x[:HD], zero], axis=0)
    right = jnp.concatenate([zero, x[HD:]], axis=0)
    return jnp.concatenate([left, right], axis=1)


def near_attention(heads_dev, npair, ids, first_kv, rest):
    wide = rest[0].shape[1]
    per = wide // BLK
    nblk = npair * per
    feats = heads_dev * HD
    low_q = (heads_dev - 1) * 2 * HD
    cols = heads_dev * BLK
    keys = NEAR * BLK

    def body(ids_ref, *refs):
        tabs = refs[:npair]
        rests = refs[npair : 2 * npair]
        out_ref, stat_ref, kv, q, ktab, vtab, s_a, s_b, t_a, t_b, sems = refs[2 * npair :]
        pair, _, cluster, _ = place()
        base = cluster * nblk
        loads = []
        for j in range(npair):
            at = pair ^ j
            loads.append(pltpu.make_async_copy(tabs[j], kv.at[0, at], sems.at[j]))
            for h in range(1, heads_dev):
                loads.append(
                    pltpu.make_async_copy(
                        rests[j].at[pl.ds((h - 1) * 2 * HD, 2 * HD)], kv.at[h, at], sems.at[h * npair + j]
                    )
                )
            loads.append(
                pltpu.make_async_copy(
                    rests[j].at[pl.ds(low_q, feats)], q.at[at], sems.at[heads_dev * npair + j]
                )
            )
        for load in loads:
            load.start()
        for load in loads:
            load.wait()

        def build(p, carry):
            for i in range(per):
                at = slice(i * BLK, (i + 1) * BLK)
                pieces = [kv[h, p, :, at] for h in range(heads_dev)]
                if heads_dev == 1:
                    ktab[p * per + i] = pieces[0].T
                else:
                    ktab[p * per + i] = jnp.concatenate([x[:HD] for x in pieces], axis=0).T
                vtab[p * per + i] = jnp.concatenate([x[HD:] for x in pieces], axis=0)
            return carry

        lax.fori_loop(0, npair, build, 0)

        def scores(b, qm, held, c, best):
            for j in range(c, c + 4):
                s = jnp.dot(ktab[ids_ref[j, b] - base], qm, preferred_element_type=F32)
                held[j * BLK : (j + 1) * BLK, :] = s
                part = jnp.max(s.reshape(BLK // 8, 8, cols), axis=0)
                best = part if best is None else jnp.maximum(best, part)
            return best

        def values(b, held, top, c, acc, total):
            p = jnp.exp2((held[c * BLK : (c + 4) * BLK, :] - top) * LOG2E)
            part = jnp.sum(p.reshape(4 * BLK // 8, 8, cols), axis=0)
            v = jnp.concatenate([vtab[ids_ref[c + i, b] - base] for i in range(4)], axis=1)
            o = jnp.dot(v, p.astype(BF16), preferred_element_type=F32)
            return (o, part) if acc is None else (acc + o, total + part)

        def stage(start, held, top_ref, held_after, top_after):
            for u in range(NEAR_UNROLL):
                b = start + u
                after = jnp.minimum(b + NEAR_UNROLL, nblk - 1)
                qm = query_matrix(heads_dev, q, per, after)
                top = top_ref[u]
                acc = total = best = None
                for c in range(0, NEAR, 4):
                    best = scores(after, qm, held_after.at[u], c, best)
                    acc, total = values(b, held.at[u], top, c, acc, total)
                top_after[u] = jnp.max(best, axis=0, keepdims=True)
                out_ref[b] = jnp.concatenate(
                    [acc[h * HD : (h + 1) * HD, h * BLK : (h + 1) * BLK] for h in range(heads_dev)],
                    axis=0,
                )
                stat_ref[b, 0:1, :] = top
                stat_ref[b, 1:2, :] = jnp.sum(total, axis=0, keepdims=True)

        for u in range(NEAR_UNROLL):
            qm = query_matrix(heads_dev, q, per, u)
            best = None
            for c in range(0, NEAR, 4):
                best = scores(u, qm, s_a.at[u], c, best)
            t_a[u] = jnp.max(best, axis=0, keepdims=True)

        def step(n, carry):
            b = n * NEAR_UNROLL
            pl.when(lax.rem(n, 2) == 0)(lambda: stage(b, s_a, t_a, s_b, t_b))
            pl.when(lax.rem(n, 2) == 1)(lambda: stage(b, s_b, t_b, s_a, t_a))
            return carry

        lax.fori_loop(0, nblk // NEAR_UNROLL, step, 0)

    flops = nblk * keys * BLK * feats * 4 * heads_dev
    return pl.pallas_call(
        body,
        out_shape=[
            jax.ShapeDtypeStruct((nblk, feats, BLK), F32),
            jax.ShapeDtypeStruct((nblk, 8, cols), F32),
        ],
        in_specs=[SMEM] + [ANY] * (2 * npair),
        out_specs=[VMEM, VMEM],
        scratch_shapes=[
            pltpu.VMEM((heads_dev, npair, 2 * HD, wide), BF16),
            pltpu.VMEM((npair, feats, wide), BF16),
            pltpu.VMEM((nblk, BLK, 2 * HD), BF16),
            pltpu.VMEM((nblk, feats, BLK), BF16),
            pltpu.VMEM((NEAR_UNROLL, keys, cols), F32),
            pltpu.VMEM((NEAR_UNROLL, keys, cols), F32),
            pltpu.VMEM((NEAR_UNROLL, 1, cols), F32),
            pltpu.VMEM((NEAR_UNROLL, 1, cols), F32),
            pltpu.SemaphoreType.DMA((npair * (heads_dev + 1),)),
        ],
        compiler_params=params(40),
        cost_estimate=cost(2 * flops, 8 * nblk * BLK * feats, nblk * keys * cols),
        name="near_attention",
    )(ids, *first_kv, *rest)


def far_attention(heads_dev, npair, seq_size, ncl, cap, pos, tables, rest, near, stats):
    wide = rest[0].shape[1]
    per = wide // BLK
    nblk = npair * per
    low_q = (heads_dev - 1) * 2 * HD
    dev_blocks = nblk // seq_size
    feats = heads_dev * HD
    cols = heads_dev * BLK
    keys = REMOTE * BLK
    shifts = ncl - 1

    def body(pos_ref, *refs):
        tabs = refs[: heads_dev * shifts]
        refs = refs[heads_dev * shifts :]
        rests = refs[:npair]
        near_ref, stat_ref = refs[npair : npair + 2]
        outs = refs[npair + 2 : npair + 2 + seq_size]
        kv, q, ktab, vtab, old, s_a, s_b, t_a, t_b, att, sems = refs[npair + 2 + seq_size :]
        pair, _, cluster, seq = place()
        loads = []
        for h in range(heads_dev):
            for s in range(shifts):
                origin = lax.rem(cluster + ncl - 1 - s, ncl) * cap
                n = h * shifts + s
                loads.append(pltpu.make_async_copy(tabs[n], kv.at[h, pl.ds(origin, cap)], sems.at[n]))
        for j in range(npair):
            loads.append(
                pltpu.make_async_copy(
                    rests[j].at[pl.ds(low_q, feats)], q.at[pair ^ j], sems.at[heads_dev * shifts + j]
                )
            )
        late = []
        for k in range(seq_size):
            at = pl.ds((seq ^ k) * dev_blocks, dev_blocks)
            late.append(
                pltpu.make_async_copy(near_ref.at[at], old.at[at], sems.at[heads_dev * shifts + npair + k])
            )
        for load in loads + late:
            load.start()
        for load in loads:
            load.wait()

        def build(s, carry):
            origin = lax.rem(cluster + ncl - s, ncl) * cap
            for i in range(cap):
                pieces = [kv[h, origin + i] for h in range(heads_dev)]
                if heads_dev == 1:
                    ktab[origin + i] = pieces[0].T
                else:
                    ktab[origin + i] = jnp.concatenate([x[:HD] for x in pieces], axis=0).T
                vtab[origin + i] = jnp.concatenate([x[HD:] for x in pieces], axis=0)
            return carry

        lax.fori_loop(1, ncl, build, 0)

        for load in late:
            load.wait()

        def block_of(n):
            return (seq ^ (n // dev_blocks)) * dev_blocks + lax.rem(n, dev_blocks)

        def scores(b, qm, held, c, best):
            valid = pos_ref[REMOTE, b] - NEAR
            for j in range(c, c + 4):
                s = jnp.dot(ktab[pos_ref[j, b]], qm, preferred_element_type=F32)
                if j:
                    s = jnp.where(j < valid, s, -1e30)
                held[j * BLK : (j + 1) * BLK, :] = s
                part = jnp.max(s.reshape(BLK // 8, 8, cols), axis=0)
                best = part if best is None else jnp.maximum(best, part)
            return best

        def values(b, held, top, c, acc, total):
            p = jnp.exp2((held[c * BLK : (c + 4) * BLK, :] - top) * LOG2E)
            part = jnp.sum(p.reshape(4 * BLK // 8, 8, cols), axis=0)
            v = jnp.concatenate([vtab[pos_ref[c + i, b]] for i in range(4)], axis=1)
            o = jnp.dot(v, p.astype(BF16), preferred_element_type=F32)
            return (o, part) if acc is None else (acc + o, total + part)

        def stage(start, held, top_ref, held_after, top_after):
            for u in range(FAR_UNROLL):
                n = start + u
                b = block_of(n)
                after = block_of(jnp.minimum(n + FAR_UNROLL, nblk - 1))
                qm = query_matrix(heads_dev, q, per, after)
                was = stat_ref[b, 0:1, :]
                top = jnp.maximum(was, top_ref[u])
                acc = total_f = best = None
                for c in range(0, REMOTE, 4):
                    best = scores(after, qm, held_after.at[u], c, best)
                    acc, total_f = values(b, held.at[u], top, c, acc, total_f)
                top_after[u] = jnp.max(best, axis=0, keepdims=True)
                fade = jnp.exp2((was - top) * LOG2E)
                inv = 1.0 / (stat_ref[b, 1:2, :] * fade + jnp.sum(total_f, axis=0, keepdims=True))
                kept = fade * inv
                res = []
                for h in range(heads_dev):
                    at, lane = slice(h * HD, (h + 1) * HD), slice(h * BLK, (h + 1) * BLK)
                    res.append(acc[at, lane] * inv[:, lane] + old[b, at, :] * kept[:, lane])
                att[n] = jnp.concatenate(res, axis=0).astype(BF16)

        for u in range(FAR_UNROLL):
            b = block_of(u)
            qm = query_matrix(heads_dev, q, per, b)
            best = None
            for c in range(0, REMOTE, 4):
                best = scores(b, qm, s_a.at[u], c, best)
            t_a[u] = jnp.max(best, axis=0, keepdims=True)

        def step(i, carry):
            n = i * FAR_UNROLL
            pl.when(lax.rem(i, 2) == 0)(lambda: stage(n, s_a, t_a, s_b, t_b))
            pl.when(lax.rem(i, 2) == 1)(lambda: stage(n, s_b, t_b, s_a, t_a))
            return carry

        lax.fori_loop(0, nblk // FAR_UNROLL, step, 0)
        for k in range(seq_size):
            for i in range(dev_blocks):
                outs[k][:, i * BLK : (i + 1) * BLK] = att[k * dev_blocks + i]

    flops = nblk * keys * BLK * feats * 4 * heads_dev
    return pl.pallas_call(
        body,
        out_shape=[jax.ShapeDtypeStruct((feats, dev_blocks * BLK), BF16)] * seq_size,
        in_specs=[SMEM] + [ANY] * (heads_dev * shifts + npair) + [ANY, VMEM],
        out_specs=[VMEM] * seq_size,
        scratch_shapes=[
            pltpu.VMEM((heads_dev, ncl * cap, 2 * HD, BLK), BF16),
            pltpu.VMEM((npair, feats, wide), BF16),
            pltpu.VMEM((ncl * cap, BLK, 2 * HD), BF16),
            pltpu.VMEM((ncl * cap, feats, BLK), BF16),
            pltpu.VMEM((nblk, feats, BLK), F32),
            pltpu.VMEM((FAR_UNROLL, keys, cols), F32),
            pltpu.VMEM((FAR_UNROLL, keys, cols), F32),
            pltpu.VMEM((FAR_UNROLL, 1, cols), F32),
            pltpu.VMEM((FAR_UNROLL, 1, cols), F32),
            pltpu.VMEM((nblk, feats, BLK), BF16),
            pltpu.SemaphoreType.DMA((heads_dev * shifts + npair + seq_size,)),
        ],
        compiler_params=params(40),
        cost_estimate=cost(flops, 6 * nblk * BLK * feats, nblk * keys * cols),
        name="far_attention",
    )(pos, *[x for t in tables for x in t], *rest, near, stats)


def project_out(seq_size, pieces, w_out):
    feats, rows = pieces[0].shape
    step = 128

    def body(*refs):
        parts = refs[:seq_size]
        w_ref, out_ref, at, out, sems = refs[seq_size:]
        seq = place()[3]
        loads = []
        for k in range(seq_size):
            row = pl.multiple_of((seq ^ k) * feats, feats)
            loads.append(pltpu.make_async_copy(parts[k], at.at[pl.ds(row, feats)], sems.at[k]))
        for load in loads:
            load.start()
        for load in loads:
            load.wait()
        stores = []
        for n, r in enumerate(range(0, rows, step)):
            out[r : r + step, :] = jnp.dot(
                at[:, r : r + step].T, w_ref[...], preferred_element_type=F32
            ).astype(BF16)
            rows_at = pl.ds(r, step)
            stores.append(pltpu.make_async_copy(out.at[rows_at], out_ref.at[rows_at], sems.at[seq_size + n]))
            stores[-1].start()
        for store in stores:
            store.wait()

    return pl.pallas_call(
        body,
        out_shape=jax.ShapeDtypeStruct((rows, D), BF16),
        in_specs=[ANY] * seq_size + [VMEM],
        out_specs=ANY,
        scratch_shapes=[
            pltpu.VMEM((HEADS * HD, rows), BF16),
            pltpu.VMEM((rows, D), BF16),
            pltpu.SemaphoreType.DMA((seq_size + rows // step,)),
        ],
        compiler_params=params(40),
        cost_estimate=cost(2 * rows * D * D, 2 * D * D + 4 * rows * D),
        name="project_out",
    )(*pieces, w_out)


def shifted(x, axis, size, shift):
    return lax.ppermute(x, axis, [(i, (i + shift) % size) for i in range(size)])


def crossed(x, size, k):
    return lax.ppermute(x, "seq", [(i, i ^ k) for i in range(size)])


def block_lists(ncl, nblk, slots, counts):
    cap = nblk // 4

    def body(slots_ref, counts_ref, pos_ref, wanted_ref):
        valid = [counts_ref[...] > NEAR + j for j in range(REMOTE)]
        ids = [slots_ref[NEAR + j : NEAR + j + 1, :] for j in range(REMOTE)]
        spot = [jnp.zeros((1, nblk), F32) for _ in range(REMOTE)]
        row = lax.broadcasted_iota(jnp.int32, (nblk, nblk), 0)
        before = (row >= lax.broadcasted_iota(jnp.int32, (nblk, nblk), 1)).astype(F32)
        local = lax.broadcasted_iota(jnp.int32, (nblk, 128), 0).astype(F32)
        lane = lax.broadcasted_iota(jnp.int32, (nblk, 128), 1).astype(F32)
        for c in range(ncl):
            hits = [ids[j] - c * nblk == row for j in range(REMOTE)]
            named = jnp.zeros((nblk, nblk), F32)
            for j in range(REMOTE):
                named = jnp.maximum(named, jnp.where(hits[j] & valid[j], 1.0, 0.0))
            present = jnp.max(named, axis=1, keepdims=True)
            wide = jnp.broadcast_to(present, (nblk, 128))
            rank = jnp.dot(before, wide, preferred_element_type=F32) - 1.0
            chosen = jnp.sum(jnp.where((rank == lane) & (wide > 0.0), local, 0.0), axis=0, keepdims=True)
            wanted_ref[c] = jnp.broadcast_to(chosen, (8, 128)).astype(jnp.int32)
            place = rank[:, :nblk] + float(c * cap)
            for j in range(REMOTE):
                spot[j] = spot[j] + jnp.sum(jnp.where(hits[j], place, 0.0), axis=0, keepdims=True)
        for j in range(REMOTE):
            pos_ref[j : j + 1, :] = jnp.where(valid[j], spot[j], spot[0]).astype(jnp.int32)
        pos_ref[REMOTE:, :] = counts_ref[...]

    return pl.pallas_call(
        body,
        out_shape=[
            jax.ShapeDtypeStruct((REMOTE + 1, nblk), jnp.int32),
            jax.ShapeDtypeStruct((ncl, 8, 128), jnp.int32),
        ],
        in_specs=[VMEM, VMEM],
        out_specs=[VMEM, VMEM],
        compiler_params=params(40),
        cost_estimate=cost(0, 4096),
        name="block_lists",
    )(slots, counts.reshape(1, nblk))


def farthest_first(n):
    return sorted(range(1, n), key=lambda k: (-bin(k).count("1"), k))


def exchange(parts, earlier, seq_size):
    parts = list(parts)
    if earlier is not None:
        parts[1], earlier[-1] = lax.optimization_barrier((parts[1], earlier[-1]))
    for j in farthest_first(len(parts)):
        parts[j] = crossed(parts[j], seq_size, 2 * j)
    return parts


def on_device(nodes, w_qkv, w_out, kv_ids, counts):
    seq_size = lax.axis_size("seq")
    ncl = lax.axis_size("cluster")
    heads_dev = HEADS // seq_size
    npair = seq_size // 2
    nblk = seq_size * nodes.shape[0] // BLK
    cap = nblk // 4
    other = crossed(nodes, seq_size, 1)
    slots = kv_ids.T
    pos, wanted = block_lists(ncl, nblk, slots, counts)
    q_span = [(3 * h * HD, HD) for h in range(heads_dev)]
    spans = [[((3 * h + 1) * HD, 2 * HD)] for h in range(heads_dev)]
    (first_kv,) = project(spans[:1], heads_dev, npair, nodes, other, w_qkv)
    wanted, first_kv[0] = lax.optimization_barrier((wanted, first_kv[0]))
    asked = lax.all_to_all(wanted, "cluster", split_axis=0, concat_axis=0, tiled=True)
    (rest,) = project([sum(spans[1:] + [q_span], [])], heads_dev, npair, nodes, other, w_qkv)
    asked, rest = lax.optimization_barrier((asked, rest))
    first_kv = exchange(first_kv, None, seq_size)
    rest = exchange(rest, first_kv, seq_size)
    far = []
    for h in range(heads_dev):
        tables, row = (first_kv, 0) if h == 0 else (rest, (h - 1) * 2 * HD)
        picked = list(select(npair, ncl, cap, asked, tables, row))
        order = sorted(range(ncl - 1), key=lambda s: (abs(2 * s + 2 - ncl), -s))
        last = order[-1]
        if h:
            picked[last], far[h - 1][order[1]] = lax.optimization_barrier((picked[last], far[h - 1][order[1]]))
        else:
            picked[last], rest[-1] = lax.optimization_barrier((picked[last], rest[-1]))
        for s in order:
            picked[s] = shifted(picked[s], "cluster", ncl, s + 1)
        far.append(picked)
    near, stats = near_attention(heads_dev, npair, slots, first_kv, rest)
    outs = far_attention(
        heads_dev, npair, seq_size, ncl, cap, pos, far, rest, near, stats
    )
    pieces = list(outs)
    for k in sorted(range(1, seq_size), key=lambda k: (-bin(k // 2).count("1"), k)):
        pieces[k] = crossed(pieces[k], seq_size, k)
    return project_out(seq_size, pieces, w_out)


def solution(mesh):
    placed = (P(("cluster", "seq"), None), P(), P(), P("cluster", None), P("cluster"))
    return jax.shard_map(
        on_device,
        mesh=mesh,
        in_specs=placed,
        out_specs=P(("cluster", "seq"), None),
        check_vma=False,
    )
```
